512 devices in a mesh: head: 8 (over x, core), ctx: 64 (over z, y).
Axes of the slice: x: 4, y: 4, z: 16, core: 2. Of those that a mesh axis runs over, the one named last changes fastest.
Arguments:
- queries: bfloat16 [32768, 32, 128], P('ctx', 'head'), may hold values from -1.75 to 1.75
- keys: bfloat16 [32768, 32, 128], P('ctx', 'head'), may hold values from -1.75 to 1.75
- values: bfloat16 [32768, 32, 128], P('ctx', 'head'), may hold values from -6 to 6
- out_grad: bfloat16 [32768, 32, 128], P('ctx', 'head'), may hold values from -6 to 6
- gain: float32 [32, 128], P('head'), may hold values from 0.25 to 1.75
- decay_rate: float32 [32], P('head'), may hold values from 1e-05 to 0.03
- doc_lengths: int32 [128], replicated, may hold values from 1 to 4096, 32768 in all
Outputs:
- q_grad: bfloat16 [32768, 32, 128], P('ctx', 'head')
- k_grad: bfloat16 [32768, 32, 128], P('ctx', 'head')
- v_grad: bfloat16 [32768, 32, 128], P('ctx', 'head')
The draws below stay inside these ranges and needn't reach their ends.
Inputs may be any that keep to these rules, and one draw needn't show every extreme that they name: `doc_lengths`: the lengths sum to 32768 and the longest is exactly 4096.
All inputs are finite; a program needn't handle non-finite values.
Results may differ from the reference program's by a relative error of at most 0.006.
Values sent between devices are 32-bit elements; how exact they have to be, the bound alone decides.
A program may use at most 64 MiB of HBM per device.

```python
import math
from functools import partial
import jax
import jax.numpy as jnp
import numpy as np
from jax import lax

HEADS = 32
HEAD_DIM = 128
TOK_DEV = 512
TOKENS = 32768
NDOCS = 128
MOST = 4096


def draw_decay_rate(key, part):
    pick_key, slow_key, fast_key = jax.random.split(key, 3)
    share = 0.5
    slow_heads = jax.random.uniform(pick_key, (HEADS,), jnp.float32) < share
    slow_rates = jnp.exp(jax.random.uniform(slow_key, (HEADS,), jnp.float32, jnp.log(1e-05), jnp.log(0.0002)))
    fast_rates = jnp.exp(jax.random.uniform(fast_key, (HEADS,), jnp.float32, jnp.log(0.002), jnp.log(0.03)))
    return jnp.where(slow_heads, slow_rates, fast_rates).astype(jnp.float32)


def block_levels(key, extent, cuts, smallest, largest):
    level = 1.0
    for axis_at, parts in cuts:
        heights = jax.random.uniform(jax.random.fold_in(jax.random.fold_in(key, 6), axis_at), (parts,), jnp.float32, smallest / len(cuts), largest / len(cuts))
        level = level * jnp.repeat(jnp.exp(heights), extent[axis_at] // parts).reshape((-1,) + (1,) * (len(extent) - 1 - axis_at))
    return level


def profile(count, total, bound, skew):
    weights = [(1 << 20) // math.isqrt(rank ** skew) + 1 for rank in range(2, count + 1)]
    spare, given = total - bound - (count - 1), [1] * (count - 1)
    while spare > 0:
        free = [i for i in range(count - 1) if given[i] < bound]
        pool, remaining = sum([weights[i] for i in free]), spare
        for i in free:
            addition = min(bound - given[i], max(1, remaining * weights[i] // pool), spare)
            given[i] = given[i] + addition
            spare = spare - addition
    return np.array([bound] + given)


def ragged(own_key, amount, total, limit, skew):
    if amount == 2:
        one = jax.random.randint(own_key, (), max(1, total - limit), min(limit, total - 1) + 1)
        return jnp.stack([one, total - one])
    sizes = jnp.asarray(profile(amount, total, limit, skew), jnp.int32)
    couples = (amount - 1) // 2
    giver, receiver = sizes[1:1 + 2 * couples:2], sizes[2:2 + 2 * couples:2]
    margin = jnp.minimum(giver - 1, limit - receiver)
    shifted = jax.random.randint(jax.random.fold_in(own_key, 1), (couples,), 0, 1 << 20) % (margin + 1)
    sizes = sizes.at[1:1 + 2 * couples:2].set(giver - shifted).at[2:2 + 2 * couples:2].set(receiver + shifted)
    return sizes[jax.random.permutation(jax.random.fold_in(own_key, 2), amount)]


def centred(stream_key, dims, width, most, cuts=(), kind=jnp.bfloat16):
    result = width * jax.random.normal(stream_key, dims, jnp.float32)
    if cuts:
        result = result * block_levels(stream_key, dims, cuts, -0.22, 0.18)
    return jnp.clip(result, -most, most).astype(kind)


def setup_inputs(seed: int = 0) -> dict:
    streams_of = jax.random.split(jax.random.key(seed), 8)
    return {
        "queries": centred(streams_of[0], (TOKENS, HEADS, HEAD_DIM), 0.3, 1.75, ((0, 64), (1, 8))),
        "keys": centred(streams_of[1], (TOKENS, HEADS, HEAD_DIM), 0.3, 1.75, ((0, 64), (1, 8))),
        "values": centred(streams_of[2], (TOKENS, HEADS, HEAD_DIM), 1.0, 6.0, ((0, 64), (1, 8))),
        "out_grad": centred(streams_of[3], (TOKENS, HEADS, HEAD_DIM), 1.0, 6.0, ((0, 64), (1, 8))),
        "gain": jnp.clip(1.0 + 0.15 * jax.random.normal(streams_of[4], (HEADS, HEAD_DIM), jnp.float32), 0.25, 1.75),
        "decay_rate": draw_decay_rate(jax.random.fold_in(streams_of[7], 71), 0),
        "doc_lengths": ragged(streams_of[6], NDOCS, TOKENS, MOST, 2).astype(jnp.int32),
    }


epsilon = 1e-06

def mix(form, left, right):
    return jnp.einsum(form, left.astype(jnp.float32), right.astype(jnp.float32), preferred_element_type=jnp.float32, precision=lax.Precision.HIGHEST)

def decay_mask(segment, decays):
    block_len = segment.shape[0]
    offsets = jnp.arange(block_len, dtype=jnp.int32)
    distance = offsets[:, None] - offsets[None, :]
    allowed = (distance >= 0) & (segment[:, None] == segment[None, :])
    weight = jnp.exp(-decays[:, None, None] * jnp.maximum(distance, 0).astype(jnp.float32)[None])
    return jnp.where(allowed[None], weight, jnp.float32(0.0))

def forward_block(decays, carry, block):
    carried, prev_seg = carry
    queries_blk, key_blk, values_blk, segment = block
    block_len = segment.shape[0]
    offsets = jnp.arange(block_len, dtype=jnp.float32)
    weight = decay_mask(segment, decays)
    scores = mix('thd,shd->hts', queries_blk, key_blk)
    weighted = (scores * weight).astype(jnp.bfloat16)
    output = mix('hts,shd->thd', weighted, values_blk)
    in_factor = jnp.where((segment == prev_seg)[:, None], jnp.exp(-decays[None, :] * (offsets[:, None] + 1.0)), jnp.float32(0.0))
    output = output + in_factor[:, :, None] * mix('thd,hde->the', queries_blk, carried.astype(jnp.bfloat16))
    last_seg = segment[-1]
    tail = jnp.where((segment == last_seg)[:, None], jnp.exp(-decays[None, :] * (block_len - 1.0 - offsets)[:, None]), jnp.float32(0.0))
    own_part = mix('shd,she->hde', (key_blk * tail[:, :, None]).astype(jnp.bfloat16), values_blk)
    keep_factor = jnp.where(prev_seg == last_seg, jnp.exp(-decays * block_len), jnp.float32(0.0))
    return ((keep_factor[:, None, None] * carried + own_part, last_seg), (output, carried))

def gradient_block(decays, block):
    queries_blk, key_blk, values_blk, grad_blk, segment, carried, prev_seg = block
    block_len = segment.shape[0]
    offsets = jnp.arange(block_len, dtype=jnp.float32)
    weight = decay_mask(segment, decays)
    scores = mix('thd,shd->hts', queries_blk, key_blk)
    weighted = (scores * weight).astype(jnp.bfloat16)
    grad_scores = mix('thd,shd->hts', grad_blk, values_blk)
    grad_weights = (grad_scores * weight).astype(jnp.bfloat16)
    q_part = mix('hts,shd->thd', grad_weights, key_blk)
    k_part = mix('hts,thd->shd', grad_weights, queries_blk)
    v_part = mix('hts,thd->shd', weighted, grad_blk)
    in_factor = jnp.where((segment == prev_seg)[:, None], jnp.exp(-decays[None, :] * (offsets[:, None] + 1.0)), jnp.float32(0.0))
    q_part = q_part + in_factor[:, :, None] * mix('the,hde->thd', grad_blk, carried.astype(jnp.bfloat16))
    return (q_part, k_part, v_part)

def reverse_block(decays, carry, block):
    carried, next_seg = carry
    queries_blk, key_blk, values_blk, grad_blk, segment = block
    block_len = segment.shape[0]
    offsets = jnp.arange(block_len, dtype=jnp.float32)
    in_factor = jnp.where((segment == next_seg)[:, None], jnp.exp(-decays[None, :] * (block_len - offsets[:, None])), jnp.float32(0.0))
    packed = carried.astype(jnp.bfloat16)
    k_extra = in_factor[:, :, None] * mix('she,hde->shd', values_blk, packed)
    v_extra = in_factor[:, :, None] * mix('shd,hde->she', key_blk, packed)
    first_seg = segment[0]
    lead = jnp.where((segment == first_seg)[:, None], jnp.exp(-decays[None, :] * offsets[:, None]), jnp.float32(0.0))
    own_part = mix('thd,the->hde', (queries_blk * lead[:, :, None]).astype(jnp.bfloat16), grad_blk)
    keep_factor = jnp.where(first_seg == next_seg, jnp.exp(-decays * block_len), jnp.float32(0.0))
    return ((keep_factor[:, None, None] * carried + own_part, first_seg), (k_extra, v_extra))

def in_blocks(array, blocks):
    return array.reshape((blocks, array.shape[0] // blocks) + array.shape[1:])

def reference(queries, keys, values, out_grad, gain, decay_rate, doc_lengths):
    tok_total, head_count, head_dim = queries.shape
    block_len = min(512, TOK_DEV)
    blocks = tok_total // block_len
    starts = (jnp.cumsum(doc_lengths) - doc_lengths).astype(jnp.int32)
    start_flags = jnp.zeros((tok_total,), jnp.int32).at[starts].add(1)
    segment = (jnp.cumsum(start_flags) - 1).astype(jnp.int32)
    query_b = in_blocks(queries, blocks)
    key_b = in_blocks(keys, blocks)
    value_b = in_blocks(values, blocks)
    seg_b = in_blocks(segment, blocks)
    zero_state = jnp.zeros((head_count, head_dim, head_dim), jnp.float32)
    final_carry, (outs, entry_states) = lax.scan(partial(forward_block, decay_rate), (zero_state, jnp.array(-1, jnp.int32)), (query_b, key_b, value_b, seg_b))
    attn_out = outs.reshape(tok_total, head_count, head_dim)
    gained = gain[None] * out_grad.astype(jnp.float32)
    squares = lax.optimization_barrier(jnp.sum(attn_out * attn_out, axis=(1, 2)))
    cross = lax.optimization_barrier(jnp.sum(gained * attn_out, axis=(1, 2)))
    norm_width = head_count * head_dim
    inverse = 1.0 / jnp.sqrt(squares / norm_width + epsilon)
    grad_o = (gained * inverse[:, None, None] - attn_out * (cross * inverse * inverse * inverse / norm_width)[:, None, None]).astype(jnp.bfloat16)
    grad_b = in_blocks(grad_o, blocks)
    prev_blocks = jnp.concatenate([jnp.array([-1], jnp.int32), seg_b[:-1, -1]]).astype(jnp.int32)
    q_part, k_part, v_part = lax.map(partial(gradient_block, decay_rate), (query_b, key_b, value_b, grad_b, seg_b, entry_states, prev_blocks))
    back_carry, (k_extra, v_extra) = lax.scan(partial(reverse_block, decay_rate), (zero_state, jnp.array(-2, jnp.int32)), (query_b, key_b, value_b, grad_b, seg_b), reverse=True)
    shape = (tok_total, head_count, head_dim)
    q_grad = q_part.reshape(shape)
    k_grad = (k_part + k_extra).reshape(shape)
    v_grad = (v_part + v_extra).reshape(shape)
    return (q_grad.astype(jnp.bfloat16), k_grad.astype(jnp.bfloat16), v_grad.astype(jnp.bfloat16))
```

```python
from functools import partial

import jax
import jax.numpy as jnp
from jax import lax
from jax.sharding import PartitionSpec as P

epsilon = 1e-06


def prefix(part, axis, combine, identity, reverse):
    count = lax.axis_size(axis)
    place = lax.axis_index(axis)
    ahead = count - 1 - place if reverse else place
    gathered = jax.tree.map(lambda a: lax.all_gather(a, axis), part)
    state = jax.tree.map(lambda a, e: jnp.zeros_like(a) + jnp.asarray(e, a.dtype), part, identity)

    def one(hop, state):
        source = count - 1 - hop if reverse else hop
        return combine(
            state, jax.tree.map(lambda a: lax.dynamic_index_in_dim(a, source, 0, False), gathered)
        )

    return lax.fori_loop(0, ahead, one, state)


def mix(form, left, right):
    return jnp.einsum(
        form,
        left.astype(jnp.float32),
        right.astype(jnp.float32),
        preferred_element_type=jnp.float32,
    )


def segment_of(starts, positions):
    before = (starts[None, :] <= positions[:, None]).astype(jnp.int32)
    return jnp.sum(before, axis=1) - 1


def decay_mask(segment, decays):
    block_len = segment.shape[0]
    offsets = jnp.arange(block_len, dtype=jnp.int32)
    distance = offsets[:, None] - offsets[None, :]
    allowed = (distance >= 0) & (segment[:, None] == segment[None, :])
    weight = jnp.exp(-decays[:, None, None] * jnp.maximum(distance, 0).astype(jnp.float32)[None])
    return jnp.where(allowed[None], weight, jnp.float32(0.0))


def forward_block(decays, carry, block):
    carried, prev_seg = carry
    queries_blk, key_blk, values_blk, segment = block
    block_len = segment.shape[0]
    offsets = jnp.arange(block_len, dtype=jnp.float32)
    weight = decay_mask(segment, decays)
    scores = mix("thd,shd->hts", queries_blk, key_blk)
    weighted = (scores * weight).astype(jnp.bfloat16)
    output = mix("hts,shd->thd", weighted, values_blk)
    in_factor = jnp.where(
        (segment == prev_seg)[:, None],
        jnp.exp(-decays[None, :] * (offsets[:, None] + 1.0)),
        jnp.float32(0.0),
    )
    output = output + in_factor[:, :, None] * mix(
        "thd,hde->the", queries_blk, carried.astype(jnp.bfloat16)
    )
    last_seg = segment[-1]
    tail = jnp.where(
        (segment == last_seg)[:, None],
        jnp.exp(-decays[None, :] * (block_len - 1.0 - offsets)[:, None]),
        jnp.float32(0.0),
    )
    own_part = mix("shd,she->hde", (key_blk * tail[:, :, None]).astype(jnp.bfloat16), values_blk)
    keep_factor = jnp.where(prev_seg == last_seg, jnp.exp(-decays * block_len), jnp.float32(0.0))
    return (
        (keep_factor[:, None, None] * carried + own_part, last_seg),
        (output, carried, weighted),
    )


def gradient_block(decays, block):
    queries_blk, key_blk, values_blk, grad_blk, segment, carried, prev_seg, weighted = block
    block_len = segment.shape[0]
    offsets = jnp.arange(block_len, dtype=jnp.float32)
    weight = decay_mask(segment, decays)
    grad_scores = mix("thd,shd->hts", grad_blk, values_blk)
    grad_weights = (grad_scores * weight).astype(jnp.bfloat16)
    q_part = mix("hts,shd->thd", grad_weights, key_blk)
    k_part = mix("hts,thd->shd", grad_weights, queries_blk)
    v_part = mix("hts,thd->shd", weighted, grad_blk)
    in_factor = jnp.where(
        (segment == prev_seg)[:, None],
        jnp.exp(-decays[None, :] * (offsets[:, None] + 1.0)),
        jnp.float32(0.0),
    )
    q_part = q_part + in_factor[:, :, None] * mix(
        "the,hde->thd", grad_blk, carried.astype(jnp.bfloat16)
    )
    return (q_part, k_part, v_part)


def reverse_block(decays, carry, block):
    carried, next_seg = carry
    queries_blk, key_blk, values_blk, grad_blk, segment = block
    block_len = segment.shape[0]
    offsets = jnp.arange(block_len, dtype=jnp.float32)
    in_factor = jnp.where(
        (segment == next_seg)[:, None],
        jnp.exp(-decays[None, :] * (block_len - offsets[:, None])),
        jnp.float32(0.0),
    )
    packed = carried.astype(jnp.bfloat16)
    k_extra = in_factor[:, :, None] * mix("she,hde->shd", values_blk, packed)
    v_extra = in_factor[:, :, None] * mix("shd,hde->she", key_blk, packed)
    first_seg = segment[0]
    lead = jnp.where(
        (segment == first_seg)[:, None],
        jnp.exp(-decays[None, :] * offsets[:, None]),
        jnp.float32(0.0),
    )
    own_part = mix("thd,the->hde", (queries_blk * lead[:, :, None]).astype(jnp.bfloat16), grad_blk)
    keep_factor = jnp.where(first_seg == next_seg, jnp.exp(-decays * block_len), jnp.float32(0.0))
    return ((keep_factor[:, None, None] * carried + own_part, first_seg), (k_extra, v_extra))


def in_blocks(array, blocks):
    return array.reshape((blocks, array.shape[0] // blocks) + array.shape[1:])


def chain_combine(earlier, latter):
    return (earlier[0] * latter[0], latter[0][:, None, None] * earlier[1] + latter[1])


def local(queries, keys, values, out_grad, gain, decay_rate, doc_lengths):
    tok_rows, head_count, head_dim = queries.shape
    block_len = min(512, tok_rows)
    blocks = tok_rows // block_len
    norm_width = head_count * head_dim * lax.axis_size("head")
    first_row = lax.axis_index("ctx") * tok_rows
    order = jnp.arange(doc_lengths.shape[0], dtype=jnp.int32)
    starts = jnp.sum(jnp.where(order[None, :] < order[:, None], doc_lengths[None, :], 0), axis=1)
    positions = first_row + jnp.arange(tok_rows, dtype=jnp.int32)
    segment = segment_of(starts, positions)
    prev_seg = segment_of(starts, jnp.reshape(first_row - 1, (1,)))[0]
    next_seg = segment_of(starts, jnp.reshape(first_row + tok_rows, (1,)))[0]
    offsets = jnp.arange(tok_rows, dtype=jnp.float32)
    query_b = in_blocks(queries, blocks)
    key_b = in_blocks(keys, blocks)
    value_b = in_blocks(values, blocks)
    seg_b = in_blocks(segment, blocks)
    zero_state = jnp.zeros((head_count, head_dim, head_dim), jnp.float32)
    identity = (jnp.ones((head_count,), jnp.float32), zero_state)
    shard_fade = jnp.exp(-decay_rate * tok_rows)
    (own_state, last_seg), (outs_local, entry_states, weighted_b) = lax.scan(
        partial(forward_block, decay_rate), (zero_state, prev_seg), (query_b, key_b, value_b, seg_b)
    )
    forward_summary = (jnp.where(prev_seg == segment[-1], shard_fade, jnp.float32(0.0)), own_state)
    forward_in = prefix(forward_summary, "ctx", chain_combine, identity, False)
    state_in = forward_in[1].astype(jnp.bfloat16)
    in_factor = jnp.where(
        (segment == prev_seg)[:, None],
        jnp.exp(-decay_rate[None, :] * (offsets[:, None] + 1.0)),
        jnp.float32(0.0),
    )
    attn_out = outs_local.reshape(tok_rows, head_count, head_dim)
    attn_out = attn_out + in_factor[:, :, None] * mix("thd,hde->the", queries, state_in)
    gained = gain[None] * out_grad.astype(jnp.float32)
    squares = jnp.sum(attn_out * attn_out, axis=(1, 2))
    cross = jnp.sum(gained * attn_out, axis=(1, 2))
    squares, cross = lax.psum((squares, cross), "head")
    inverse = 1.0 / jnp.sqrt(squares / norm_width + epsilon)
    grad_o = (
        gained * inverse[:, None, None]
        - attn_out * (cross * inverse * inverse * inverse / norm_width)[:, None, None]
    ).astype(jnp.bfloat16)
    grad_b = in_blocks(grad_o, blocks)
    (own_grad, first_seg), (k_extra, v_extra) = lax.scan(
        partial(reverse_block, decay_rate),
        (zero_state, next_seg),
        (query_b, key_b, value_b, grad_b, seg_b),
        reverse=True,
    )
    gradient_summary = (jnp.where(segment[0] == next_seg, shard_fade, jnp.float32(0.0)), own_grad)
    gradient_in = prefix(gradient_summary, "ctx", chain_combine, identity, True)
    prev_blocks = jnp.concatenate([jnp.reshape(prev_seg, (1,)), seg_b[:-1, -1]])
    q_part, k_part, v_part = lax.map(
        partial(gradient_block, decay_rate),
        (query_b, key_b, value_b, grad_b, seg_b, entry_states, prev_blocks, weighted_b),
    )
    shape = (tok_rows, head_count, head_dim)
    q_grad = q_part.reshape(shape) + in_factor[:, :, None] * mix("the,hde->thd", grad_o, state_in)
    back_factor = jnp.where(
        (segment == next_seg)[:, None],
        jnp.exp(-decay_rate[None, :] * (tok_rows - offsets[:, None])),
        jnp.float32(0.0),
    )
    packed = gradient_in[1].astype(jnp.bfloat16)
    k_grad = (k_part + k_extra).reshape(shape) + back_factor[:, :, None] * mix(
        "she,hde->shd", values, packed
    )
    v_grad = (v_part + v_extra).reshape(shape) + back_factor[:, :, None] * mix(
        "shd,hde->she", keys, packed
    )
    return (q_grad.astype(jnp.bfloat16), k_grad.astype(jnp.bfloat16), v_grad.astype(jnp.bfloat16))


def solution(mesh):
    in_specs = (
        P("ctx", "head", None),
        P("ctx", "head", None),
        P("ctx", "head", None),
        P("ctx", "head", None),
        P("head", None),
        P("head"),
        P(),
    )
    out_specs = (P("ctx", "head", None), P("ctx", "head", None), P("ctx", "head", None))
    return jax.shard_map(local, mesh=mesh, in_specs=in_specs, out_specs=out_specs, check_vma=False)
```

```python
import functools

import jax
import jax.numpy as jnp
from jax import lax
from jax.experimental import pallas as pl
from jax.experimental.pallas import tpu as pltpu
from jax.sharding import PartitionSpec as P

epsilon = 1e-06
BLK = 512
GROUP = 4
FEAT = 128
HPD = 4
FAR = 1e37
f32 = jnp.float32
bf16 = jnp.bfloat16
PARTS = ((0, 256, 0), (256, 512, 256))


def nn(a, b):
    return lax.dot_general(a, b, (((1,), (0,)), ((), ())), preferred_element_type=f32)


def nt(a, b):
    return lax.dot_general(a, b, (((1,), (1,)), ((), ())), preferred_element_type=f32)


def kernel(
    zs, hs, total, width,
    q_hbm, k_hbm, v_hbm, g_hbm, gain_ref, rate_ref, lens_ref,
    qo_hbm, ko_hbm, vo_hbm,
    qin, kin, vin, gin, st_q, st_k, st_v, st_g,
    qh, kh, vh, qT, kT, vT, gT, dist, decay, probsT, oT, goT,
    fown, frec, fsum, fin, fout, fent,
    bown, brec, bsum, bin_, bout, bent,
    stat, stats, kacc, vacc, backc, so_q, so_k, so_v, oq, ok, ov,
    in_sem, out_sem, a_s, a_r, t_s, t_r, e_s, e_r, n_s, n_r, c_s, c_r, u_s, u_r, w_s, w_r,
):
    head = lax.axis_index("head")
    ctx = lax.axis_index("ctx")
    z = ctx // GROUP
    y = ctx % GROUP

    def row_dev(d):
        return {"ctx": z * GROUP + (y + d) % GROUP}

    def col_dev(d):
        return {"ctx": ((z + d + zs) % zs) * GROUP + y}

    def head_dev(m):
        return {"head": (head + m) % hs}

    loads = [
        pltpu.make_async_copy(s, t, in_sem.at[i])
        for i, (s, t) in enumerate(((k_hbm, kin), (v_hbm, vin), (q_hbm, qin), (g_hbm, gin)))
    ]
    for c in loads:
        c.start()
    barrier = pltpu.get_barrier_semaphore()
    peers = [row_dev(d) for d in range(1, GROUP)]
    peers += [col_dev(d) for d in (-2, -1, 1, 2)]
    peers += [head_dev(m) for m in range(1, hs)]
    for p in peers:
        pl.semaphore_signal(barrier, inc=1, device_id=p, device_id_type=pl.DeviceIdType.MESH)

    b0 = (ctx * BLK).astype(f32)
    g0 = (z * (BLK * GROUP)).astype(f32)
    lens = jnp.broadcast_to(lens_ref[...].astype(f32), (128, 128))
    low = lax.broadcasted_iota(jnp.int32, (128, 128), 0) < lax.broadcasted_iota(jnp.int32, (128, 128), 1)
    starts = jnp.sum(jnp.where(low, lens.T, 0.0), axis=0, keepdims=True)
    starts_c = jnp.broadcast_to(starts, (128, 128)).T
    t_row = lax.broadcasted_iota(jnp.int32, (1, BLK), 1).astype(f32)
    own_start = jnp.concatenate(
        [
            jnp.max(
                jnp.where(starts_c - b0 <= t_row[:, i : i + 128], starts_c - b0, -2.0 * total),
                axis=0, keepdims=True,
            )
            for i in range(0, BLK, 128)
        ],
        axis=1,
    )

    def start_of(position):
        found = jnp.max(jnp.where(starts <= position, starts, -1.0), axis=1, keepdims=True)
        found = jnp.broadcast_to(found, (8, 128))
        return jnp.where(position >= total, f32(total), found)

    idx = lax.broadcasted_iota(jnp.int32, (8, 128), 0)
    idxf = idx.astype(f32)
    ends = start_of(jnp.where(idx == 5, b0 + (BLK - 1.0), g0 + idxf * BLK - 1.0))
    firsts = start_of(jnp.where(idx == 5, b0 + BLK, jnp.where(idx == 6, g0 + 2.0 * BLK * GROUP, g0 + idxf * BLK)))
    end_g = ends - g0
    first_g = firsts - g0
    last_start = ends[5:6, 0:1] - b0
    next_start = firsts[5:6, :] - b0

    rate_y = rate_ref[0, y]
    in_mask = own_start < 0.0
    tail_mask = t_row >= last_start
    lead_mask = own_start <= 0.0

    def in_row(h):
        return jnp.where(in_mask, jnp.exp(-rate_ref[0, h] * (t_row + 1.0)), 0.0)

    def split_heads(source, stage):
        stage[...] = source[...].astype(f32)

    def of_head(stage, h):
        return stage[pl.ds(h, BLK, stride=HPD), :]

    loads[0].wait()
    split_heads(kin, st_k)
    loads[1].wait()
    split_heads(vin, st_v)
    a_copies = []
    for d in (1, 2, 3, 0):
        h = (y + d) % GROUP
        k_f = of_head(st_k, h)
        k_t = k_f.T
        kh[h] = k_f.astype(bf16)
        kT[h] = k_t.astype(bf16)
        v_f = of_head(st_v, h)
        vh[h] = v_f.astype(bf16)
        tail = jnp.where(tail_mask, jnp.exp(-rate_ref[0, h] * (BLK - 1.0 - t_row)), 0.0)
        fown[h] = nn((k_t * tail).astype(bf16), v_f.astype(bf16))
        if d == 1:
            pl.semaphore_wait(barrier, len(peers))
        if d:
            c = pltpu.make_async_remote_copy(
                src_ref=fown.at[h], dst_ref=frec.at[d], send_sem=a_s.at[d], recv_sem=a_r.at[d],
                device_id=row_dev(d), device_id_type=pl.DeviceIdType.MESH,
            )
            c.start()
            a_copies.append(c)

    loads[2].wait()
    split_heads(qin, st_q)
    loads[3].wait()
    split_heads(gin, st_g)
    gain_c = jnp.concatenate([gain_ref[...], jnp.zeros((FEAT - HPD, FEAT), f32)], axis=0).T

    s_col = lax.broadcasted_iota(jnp.int32, (BLK, BLK), 0).astype(f32)
    t_col = lax.broadcasted_iota(jnp.int32, (BLK, BLK), 1).astype(f32)
    dist[...] = jnp.where((s_col <= t_col) & (s_col >= own_start), t_col - s_col, FAR)

    def prepare(h):
        q_f = of_head(st_q, h)
        qh[h] = q_f.astype(bf16)
        qT[h] = q_f.T.astype(bf16)
        gT[h] = of_head(st_g, h).T * gain_c[:, h : h + 1]
        vT[h] = vh[h].astype(f32).T.astype(bf16)
        s_i = lax.broadcasted_iota(jnp.int32, (BLK, FEAT), 0).astype(f32)
        backc[h] = jnp.where(s_i >= next_start, jnp.exp(-rate_ref[0, h] * (BLK - s_i)), 0.0)

    def forward(h):
        prepare(h)
        for s0, s1, t0 in PARTS:
            w = jnp.exp(-rate_ref[0, h] * dist[s0:s1, t0:])
            decay[h, s0:s1, t0:] = w
            probsT[h, s0:s1, t0:] = (nn(kh[h, s0:s1, :], qT[h, :, t0:]) * w).astype(bf16)
        oT[h, :, 0:256] = nn(vT[h, :, 0:256], probsT[h, 0:256, 0:256])
        oT[h, :, 256:512] = nn(vT[h], probsT[h, :, 256:512])

    def fade(mask, count):
        return jnp.where(mask, jnp.exp(-rate_y * (BLK * jnp.maximum(count, 0.0))), 0.0)

    forward(0)
    for c in a_copies:
        c.wait()
    inner = [None] * (GROUP + 1)
    for d in range(GROUP):
        j = (y + GROUP - d) % GROUP
        jf = j.astype(f32)
        coef = fade((idx > j) & (end_g <= BLK * (jf + 1.0) - 1.0), idxf - 1.0 - jf)
        part = fown[y] if d == 0 else frec[d]
        for i in range(1, GROUP + 1):
            term = coef[i : i + 1, :] * part
            inner[i] = term if inner[i] is None else inner[i] + term
    fsum[...] = inner[GROUP]
    t_copies = []
    for n in (1, 0):
        c = pltpu.make_async_remote_copy(
            src_ref=fsum, dst_ref=fin.at[n], send_sem=t_s.at[n], recv_sem=t_r.at[n],
            device_id=col_dev(n + 1), device_id_type=pl.DeviceIdType.MESH,
        )
        c.start()
        t_copies.append(c)
    for i in range(1, GROUP):
        fout[i] = inner[i]

    forward(1)
    forward(2)
    for c in t_copies:
        c.wait()
    far = fade(end_g <= -BLK * GROUP - 1.0, jnp.full((8, 128), GROUP, f32))[0:1, :]
    enter = fin[0] + far * fin[1]
    carry = fade(end_g <= -1.0, idxf)
    fout[0] = enter
    for i in range(1, GROUP):
        fout[i] = fout[i] + carry[i : i + 1, :] * enter
    e_copies = []
    for d in (1, 2, 3):
        c = pltpu.make_async_remote_copy(
            src_ref=fout.at[(y + d) % GROUP], dst_ref=fent.at[y], send_sem=e_s.at[d], recv_sem=e_r.at[d],
            device_id=row_dev(d), device_id_type=pl.DeviceIdType.MESH,
        )
        c.start()
        e_copies.append(c)
    fent[y] = fout[y]
    forward(3)
    for c in e_copies:
        c.wait()

    squares = jnp.zeros((8, BLK), f32)
    cross = jnp.zeros((8, BLK), f32)
    for h in range(HPD):
        state = fent[h].T.astype(bf16)
        o = oT[h] + in_row(h) * nn(state, qT[h])
        oT[h] = o
        squares = squares + jnp.sum((o * o).reshape(FEAT // 8, 8, BLK), axis=0)
        cross = cross + jnp.sum((o * gT[h]).reshape(FEAT // 8, 8, BLK), axis=0)
    squares = jnp.sum(squares, axis=0, keepdims=True)
    cross = jnp.sum(cross, axis=0, keepdims=True)
    for i in range(4):
        stat[i : i + 1, :] = squares[:, i * 128 : (i + 1) * 128]
        stat[i + 4 : i + 5, :] = cross[:, i * 128 : (i + 1) * 128]
    n_copies = []
    for m in range(1, hs):
        c = pltpu.make_async_remote_copy(
            src_ref=stat, dst_ref=stats.at[m], send_sem=n_s.at[m], recv_sem=n_r.at[m],
            device_id=head_dev(m), device_id_type=pl.DeviceIdType.MESH,
        )
        c.start()
        n_copies.append(c)
    for c in n_copies:
        c.wait()
    both = stat[...]
    for m in range(1, hs):
        both = both + stats[m]
    inverse = 1.0 / jnp.sqrt(both[0:4, :] / width + epsilon)
    factor = both[4:8, :] * inverse * inverse * inverse / width
    inv_row = jnp.concatenate([inverse[i : i + 1, :] for i in range(4)], axis=1)
    fac_row = jnp.concatenate([factor[i : i + 1, :] for i in range(4)], axis=1)

    c_copies = []
    for d in (1, 2, 3, 0):
        h = (y + d) % GROUP
        go = (gT[h] * inv_row - oT[h] * fac_row).astype(bf16)
        goT[h] = go
        lead = jnp.where(lead_mask, jnp.exp(-rate_ref[0, h] * t_row), 0.0)
        bown[h] = nt((qT[h].astype(f32) * lead).astype(bf16), go)
        if d:
            c = pltpu.make_async_remote_copy(
                src_ref=bown.at[h], dst_ref=brec.at[d], send_sem=c_s.at[d], recv_sem=c_r.at[d],
                device_id=row_dev(d), device_id_type=pl.DeviceIdType.MESH,
            )
            c.start()
            c_copies.append(c)

    def backward(h):
        go = goT[h]
        q_t = in_row(h) * nn(fent[h].astype(bf16), go)
        w0 = (nn(vh[h, 0:256, :], go) * decay[h, 0:256, :]).astype(bf16)
        w1 = (nn(vh[h, 256:512, :], go[:, 256:]) * decay[h, 256:512, 256:]).astype(bf16)
        q0 = q_t[:, 0:256] + nn(kT[h, :, 0:256], w0[:, 0:256])
        q1 = q_t[:, 256:] + nn(kT[h, :, 0:256], w0[:, 256:]) + nn(kT[h, :, 256:], w1)
        so_q[pl.ds(h, BLK, stride=HPD), :] = jnp.concatenate([q0.T, q1.T], axis=0)
        kacc[h, 0:256, :] = nn(w0, qh[h])
        kacc[h, 256:512, :] = nn(w1, qh[h, 256:512, :])
        vacc[h, 0:256, :] = nt(probsT[h, 0:256, :], go)
        vacc[h, 256:512, :] = nt(probsT[h, 256:512, 256:], go[:, 256:])

    backward(0)
    for c in c_copies:
        c.wait()
    outer = [None] * GROUP
    group_sum = None
    for d in range(GROUP):
        j = (y + GROUP - d) % GROUP
        jf = j.astype(f32)
        first_j = jnp.sum(jnp.where(idx == j, first_g, 0.0), axis=0, keepdims=True)
        at = jnp.where(idx == 7, 0.0, idxf + 1.0)
        coef = fade((jf >= at) & (first_j <= BLK * at), jf - at)
        part = bown[y] if d == 0 else brec[d]
        for i in range(GROUP - 1):
            term = coef[i : i + 1, :] * part
            outer[i] = term if outer[i] is None else outer[i] + term
        term = coef[7:8, :] * part
        group_sum = term if group_sum is None else group_sum + term
    bsum[...] = group_sum
    u_copies = []
    for n in (1, 0):
        c = pltpu.make_async_remote_copy(
            src_ref=bsum, dst_ref=bin_.at[n], send_sem=u_s.at[n], recv_sem=u_r.at[n],
            device_id=col_dev(-(n + 1)), device_id_type=pl.DeviceIdType.MESH,
        )
        c.start()
        u_copies.append(c)
    for i in range(GROUP - 1):
        bout[i] = outer[i]
    backward(1)
    backward(2)
    for c in u_copies:
        c.wait()
    far = fade(first_g <= BLK * GROUP, jnp.full((8, 128), GROUP, f32))[6:7, :]
    enter = bin_[0] + far * bin_[1]
    carry = fade(first_g[4:5, :] <= BLK * (idxf + 1.0), GROUP - 1.0 - idxf)
    bout[GROUP - 1] = enter
    for i in range(GROUP - 1):
        bout[i] = bout[i] + carry[i : i + 1, :] * enter
    w_copies = []
    for d in (1, 2, 3):
        c = pltpu.make_async_remote_copy(
            src_ref=bout.at[(y + d) % GROUP], dst_ref=bent.at[y], send_sem=w_s.at[d], recv_sem=w_r.at[d],
            device_id=row_dev(d), device_id_type=pl.DeviceIdType.MESH,
        )
        c.start()
        w_copies.append(c)
    bent[y] = bout[y]
    backward(3)
    oq[...] = so_q[...].astype(bf16)
    q_out = pltpu.make_async_copy(oq, qo_hbm, out_sem.at[0])
    q_out.start()
    for c in w_copies:
        c.wait()
    for h in range(HPD):
        state = bent[h].astype(bf16)
        so_k[pl.ds(h, BLK, stride=HPD), :] = kacc[h] + backc[h] * nt(vh[h], state)
        so_v[pl.ds(h, BLK, stride=HPD), :] = vacc[h] + backc[h] * nn(kh[h], state)
    ok[...] = so_k[...].astype(bf16)
    k_out = pltpu.make_async_copy(ok, ko_hbm, out_sem.at[1])
    k_out.start()
    ov[...] = so_v[...].astype(bf16)
    v_out = pltpu.make_async_copy(ov, vo_hbm, out_sem.at[2])
    v_out.start()
    q_out.wait()
    k_out.wait()
    v_out.wait()


def local(zs, hs, queries, keys, values, out_grad, gain, decay_rate, doc_lengths):
    rows = BLK * HPD
    flat = [a.reshape(rows, FEAT) for a in (queries, keys, values, out_grad)]
    hbm = pl.BlockSpec(memory_space=pl.ANY)
    vmem = pl.BlockSpec(memory_space=pltpu.VMEM)
    smem = pl.BlockSpec(memory_space=pltpu.SMEM)
    V = pltpu.VMEM
    mat = (FEAT, FEAT)
    chain = [
        V((HPD,) + mat, f32), V((GROUP,) + mat, f32), V(mat, f32),
        V((2,) + mat, f32), V((GROUP,) + mat, f32), V((HPD,) + mat, f32),
    ]
    scratch = (
        [V((rows, FEAT), bf16)] * 4
        + [V((rows, FEAT), f32)] * 4
        + [V((HPD, BLK, FEAT), bf16)] * 3
        + [V((HPD, FEAT, BLK), bf16)] * 3
        + [V((HPD, FEAT, BLK), f32), V((BLK, BLK), f32), V((HPD, BLK, BLK), f32), V((HPD, BLK, BLK), bf16)]
        + [V((HPD, FEAT, BLK), f32), V((HPD, FEAT, BLK), bf16)]
        + chain + chain
        + [V((8, 128), f32), V((hs, 8, 128), f32)]
        + [V((HPD, BLK, FEAT), f32)] * 3
        + [V((rows, FEAT), f32)] * 3
        + [V((rows, FEAT), bf16)] * 3
    )
    dma = pltpu.SemaphoreType.DMA
    sems = [dma((4,)), dma((3,))]
    sems += [dma((GROUP,)), dma((GROUP,)), dma((2,)), dma((2,)), dma((GROUP,)), dma((GROUP,))]
    sems += [dma((hs,)), dma((hs,))]
    sems += [dma((GROUP,)), dma((GROUP,)), dma((2,)), dma((2,)), dma((GROUP,)), dma((GROUP,))]
    outs = pl.pallas_call(
        functools.partial(kernel, zs, hs, zs * GROUP * BLK, hs * HPD * FEAT),
        out_shape=[jax.ShapeDtypeStruct((rows, FEAT), bf16)] * 3,
        in_specs=[hbm] * 4 + [vmem, smem, vmem],
        out_specs=[hbm] * 3,
        scratch_shapes=scratch + sems,
        compiler_params=pltpu.CompilerParams(
            collective_id=0, has_side_effects=True, vmem_limit_bytes=48 * 2**20
        ),
        cost_estimate=pl.CostEstimate(flops=2 * 10**9, bytes_accessed=4 * 10**6, transcendentals=10**6),
    )(*flat, gain, decay_rate.reshape(1, HPD), doc_lengths.reshape(1, doc_lengths.shape[0]))
    return tuple(o.reshape(BLK, HPD, FEAT) for o in outs)


def solution(mesh):
    spec = P("ctx", "head", None)
    zs, hs = mesh.shape["ctx"] // GROUP, mesh.shape["head"]
    return jax.shard_map(
        functools.partial(local, zs, hs), mesh=mesh,
        in_specs=(spec,) * 4 + (P("head", None), P("head"), P()),
        out_specs=(spec,) * 3, check_vma=False,
    )
```

```python
import functools

import jax
import jax.numpy as jnp
from jax import lax
from jax.experimental import pallas as pl
from jax.experimental.pallas import tpu as pltpu
from jax.sharding import PartitionSpec as P

epsilon = 1e-06
BLK = 512
GROUP = 4
FEAT = 128
HPD = 4
FAR = 1e37
f32 = jnp.float32
bf16 = jnp.bfloat16
PARTS = ((0, 256, 0), (256, 512, 256))
CHUNKS = 4
ROWS = FEAT // CHUNKS


def nn(a, b):
    return lax.dot_general(a, b, (((1,), (0,)), ((), ())), preferred_element_type=f32)


def nt(a, b):
    return lax.dot_general(a, b, (((1,), (1,)), ((), ())), preferred_element_type=f32)


def kernel(
    zs, hs, total, width,
    q_hbm, k_hbm, v_hbm, g_hbm, gain_hbm, rate_hbm, lens_hbm,
    oq, ok, ov,
    qin, kin, vin, gin, st_q, st_k, st_v, st_g,
    qh, kh, vh, qT, kT, vT, gT, dist, decay, probsT, oT, goT,
    fown, frec, fsum, fin, fout, fent,
    bown, brec, bsum, bin_, bout, bent,
    stat, stats, kacc, vacc, backc, so_q, so_k, so_v, gain_ref, rate_ref, lens_ref,
    in_sem, a_s, a_r, t_s, t_r, e_s, e_r, n_s, n_r, c_s, c_r, u_s, u_r, w_s, w_r,
):
    head = lax.axis_index("head")
    ctx = lax.axis_index("ctx")
    z = ctx // GROUP
    y = ctx % GROUP

    def row_dev(d):
        return {"ctx": z * GROUP + (y + d) % GROUP}

    def col_dev(d):
        return {"ctx": ((z + d + zs) % zs) * GROUP + y}

    def head_dev(m):
        return {"head": (head + m) % hs}

    loads = [
        pltpu.make_async_copy(s, t, in_sem.at[i])
        for i, (s, t) in enumerate(
            (
                (k_hbm, kin), (v_hbm, vin), (q_hbm, qin), (g_hbm, gin),
                (lens_hbm, lens_ref), (rate_hbm, rate_ref), (gain_hbm, gain_ref),
            )
        )
    ]
    for c in loads:
        c.start()
    barrier = pltpu.get_barrier_semaphore()
    peers = [row_dev(d) for d in range(1, GROUP)]
    peers += [col_dev(d) for d in (-2, -1, 1, 2)]
    peers += [head_dev(m) for m in range(1, hs)]
    for p in peers:
        pl.semaphore_signal(barrier, inc=1, device_id=p, device_id_type=pl.DeviceIdType.MESH)

    def remote(source, target, sends, receives, device):
        copy = pltpu.make_async_remote_copy(
            src_ref=source, dst_ref=target, send_sem=sends, recv_sem=receives,
            device_id=device, device_id_type=pl.DeviceIdType.MESH,
        )
        copy.start()
        return copy

    def chunk(c):
        return pl.ds(c * ROWS, ROWS)

    def fade(rate, mask, count):
        return jnp.where(mask, jnp.exp(-rate * (BLK * jnp.maximum(count, 0.0))), 0.0)

    for c in loads[4:]:
        c.wait()
    b0 = (ctx * BLK).astype(f32)
    g0 = (z * (BLK * GROUP)).astype(f32)
    lens = jnp.broadcast_to(lens_ref[...].astype(f32), (128, 128))
    low = lax.broadcasted_iota(jnp.int32, (128, 128), 0) < lax.broadcasted_iota(jnp.int32, (128, 128), 1)
    starts = jnp.sum(jnp.where(low, lens.T, 0.0), axis=0, keepdims=True)
    starts_c = jnp.broadcast_to(starts, (128, 128)).T
    t_row = lax.broadcasted_iota(jnp.int32, (1, BLK), 1).astype(f32)
    own_start = jnp.concatenate(
        [
            jnp.max(
                jnp.where(starts_c - b0 <= t_row[:, i : i + 128], starts_c - b0, -2.0 * total),
                axis=0, keepdims=True,
            )
            for i in range(0, BLK, 128)
        ],
        axis=1,
    )

    def start_of(position):
        found = jnp.max(jnp.where(starts <= position, starts, -1.0), axis=1, keepdims=True)
        found = jnp.broadcast_to(found, (8, 128))
        return jnp.where(position >= total, f32(total), found)

    idx = lax.broadcasted_iota(jnp.int32, (8, 128), 0)
    idxf = idx.astype(f32)
    ends = start_of(jnp.where(idx == 5, b0 + (BLK - 1.0), g0 + idxf * BLK - 1.0))
    firsts = start_of(jnp.where(idx == 5, b0 + BLK, jnp.where(idx == 6, g0 + 2.0 * BLK * GROUP, g0 + idxf * BLK)))
    end_g = ends - g0
    first_g = firsts - g0
    last_start = ends[5:6, 0:1] - b0
    next_start = firsts[5:6, :] - b0

    rate_y = rate_ref[0, y]
    in_mask = own_start < 0.0
    tail_mask = t_row >= last_start
    lead_mask = own_start <= 0.0

    def in_row(h):
        return jnp.where(in_mask, jnp.exp(-rate_ref[0, h] * (t_row + 1.0)), 0.0)

    def split_heads(source, stage):
        stage[...] = source[...].astype(f32)

    def of_head(stage, h):
        return stage[pl.ds(h, BLK, stride=HPD), :]

    loads[0].wait()
    split_heads(kin, st_k)
    loads[1].wait()
    split_heads(vin, st_v)
    a_copies = {}
    for d in (2, 1, 3, 0):
        h = (y + d) % GROUP
        k_f = of_head(st_k, h)
        k_t = k_f.T
        kh[h] = k_f.astype(bf16)
        kT[h] = k_t.astype(bf16)
        v_f = of_head(st_v, h)
        vh[h] = v_f.astype(bf16)
        tail = jnp.where(tail_mask, jnp.exp(-rate_ref[0, h] * (BLK - 1.0 - t_row)), 0.0)
        fown[h] = nn((k_t * tail).astype(bf16), v_f.astype(bf16))
        if not a_copies:
            pl.semaphore_wait(barrier, len(peers))
        if d:
            for c in range(CHUNKS):
                a_copies[d, c] = remote(
                    fown.at[h, chunk(c)], frec.at[d, chunk(c)], a_s.at[d, c], a_r.at[d, c], row_dev(d)
                )

    loads[2].wait()
    split_heads(qin, st_q)
    loads[3].wait()
    split_heads(gin, st_g)
    gain_c = jnp.concatenate([gain_ref[...], jnp.zeros((FEAT - HPD, FEAT), f32)], axis=0).T

    s_col = lax.broadcasted_iota(jnp.int32, (BLK, BLK), 0).astype(f32)
    t_col = lax.broadcasted_iota(jnp.int32, (BLK, BLK), 1).astype(f32)
    dist[...] = jnp.where((s_col <= t_col) & (s_col >= own_start), t_col - s_col, FAR)

    def prepare(h):
        q_f = of_head(st_q, h)
        qh[h] = q_f.astype(bf16)
        qT[h] = q_f.T.astype(bf16)
        gT[h] = of_head(st_g, h).T * gain_c[:, h : h + 1]
        vT[h] = vh[h].astype(f32).T.astype(bf16)
        s_i = lax.broadcasted_iota(jnp.int32, (BLK, FEAT), 0).astype(f32)
        backc[h] = jnp.where(s_i >= next_start, jnp.exp(-rate_ref[0, h] * (BLK - s_i)), 0.0)

    def forward(h):
        prepare(h)
        for s0, s1, t0 in PARTS:
            w = jnp.exp(-rate_ref[0, h] * dist[s0:s1, t0:])
            decay[h, s0:s1, t0:] = w
            probsT[h, s0:s1, t0:] = (nn(kh[h, s0:s1, :], qT[h, :, t0:]) * w).astype(bf16)
        oT[h, :, 0:256] = nn(vT[h, :, 0:256], probsT[h, 0:256, 0:256])
        oT[h, :, 256:512] = nn(vT[h], probsT[h, :, 256:512])

    forward(0)
    forward(1)
    source = [(y + GROUP - d) % GROUP for d in range(GROUP)]
    coefs = [
        fade(
            rate_y, (idx > j) & (end_g <= BLK * (j.astype(f32) + 1.0) - 1.0), idxf - 1.0 - j.astype(f32)
        )
        for j in source
    ]
    t_copies = {}
    for c in range(CHUNKS):
        for d in (1, 3, 2):
            a_copies[d, c].wait()
        total_c = coefs[0][GROUP : GROUP + 1, :] * fown[y, chunk(c), :]
        for d in range(1, GROUP):
            total_c = total_c + coefs[d][GROUP : GROUP + 1, :] * frec[d, chunk(c), :]
        fsum[chunk(c), :] = total_c
        for n in (1, 0):
            t_copies[n, c] = remote(
                fsum.at[chunk(c)], fin.at[n, chunk(c)], t_s.at[n, c], t_r.at[n, c], col_dev(n + 1)
            )
    for i in range(1, GROUP):
        inner = coefs[0][i : i + 1, :] * fown[y]
        for d in range(1, GROUP):
            inner = inner + coefs[d][i : i + 1, :] * frec[d]
        fout[i] = inner
    forward(2)
    forward(3)
    far = fade(rate_y, end_g <= -BLK * GROUP - 1.0, jnp.full((8, 128), GROUP, f32))[0:1, :]
    carry = fade(rate_y, end_g <= -1.0, idxf)
    e_copies = {}
    for c in range(CHUNKS):
        for n in (0, 1):
            t_copies[n, c].wait()
        enter = fin[0, chunk(c), :] + far * fin[1, chunk(c), :]
        fout[0, chunk(c), :] = enter
        for i in range(1, GROUP):
            fout[i, chunk(c), :] = fout[i, chunk(c), :] + carry[i : i + 1, :] * enter
        for d in (2, 1, 3):
            e_copies[d, c] = remote(
                fout.at[(y + d) % GROUP, chunk(c)], fent.at[y, chunk(c)], e_s.at[d, c], e_r.at[d, c], row_dev(d)
            )
    fent[y] = fout[y]

    squares = jnp.zeros((8, BLK), f32)
    cross = jnp.zeros((8, BLK), f32)
    for d in (0, 1, 3, 2):
        h = source[d]
        if d:
            for c in range(CHUNKS):
                e_copies[d, c].wait()
        state = fent[h].T.astype(bf16)
        o = oT[h] + in_row(h) * nn(state, qT[h])
        oT[h] = o
        squares = squares + jnp.sum((o * o).reshape(FEAT // 8, 8, BLK), axis=0)
        cross = cross + jnp.sum((o * gT[h]).reshape(FEAT // 8, 8, BLK), axis=0)
    squares = jnp.sum(squares, axis=0, keepdims=True)
    cross = jnp.sum(cross, axis=0, keepdims=True)
    for i in range(4):
        stat[i : i + 1, :] = squares[:, i * 128 : (i + 1) * 128]
        stat[i + 4 : i + 5, :] = cross[:, i * 128 : (i + 1) * 128]
    n_copies = [
        remote(stat, stats.at[m], n_s.at[m], n_r.at[m], head_dev(m))
        for m in sorted(range(1, hs), key=lambda m: abs(m - hs // 2))
    ]
    for c in n_copies:
        c.wait()
    both = stat[...]
    for m in range(1, hs):
        both = both + stats[m]
    inverse = 1.0 / jnp.sqrt(both[0:4, :] / width + epsilon)
    factor = both[4:8, :] * inverse * inverse * inverse / width
    inv_row = jnp.concatenate([inverse[i : i + 1, :] for i in range(4)], axis=1)
    fac_row = jnp.concatenate([factor[i : i + 1, :] for i in range(4)], axis=1)

    c_copies = {}
    for d in (2, 1, 3, 0):
        h = (y + d) % GROUP
        go = (gT[h] * inv_row - oT[h] * fac_row).astype(bf16)
        goT[h] = go
        lead = jnp.where(lead_mask, jnp.exp(-rate_ref[0, h] * t_row), 0.0)
        bown[h] = nt((qT[h].astype(f32) * lead).astype(bf16), go)
        if d:
            for c in range(CHUNKS):
                c_copies[d, c] = remote(
                    bown.at[h, chunk(c)], brec.at[d, chunk(c)], c_s.at[d, c], c_r.at[d, c], row_dev(d)
                )

    def backward(h):
        go = goT[h]
        q_t = in_row(h) * nn(fent[h].astype(bf16), go)
        w0 = (nn(vh[h, 0:256, :], go) * decay[h, 0:256, :]).astype(bf16)
        w1 = (nn(vh[h, 256:512, :], go[:, 256:]) * decay[h, 256:512, 256:]).astype(bf16)
        q0 = q_t[:, 0:256] + nn(kT[h, :, 0:256], w0[:, 0:256])
        q1 = q_t[:, 256:] + nn(kT[h, :, 0:256], w0[:, 256:]) + nn(kT[h, :, 256:], w1)
        so_q[pl.ds(h, BLK, stride=HPD), :] = jnp.concatenate([q0.T, q1.T], axis=0)
        kacc[h, 0:256, :] = nn(w0, qh[h])
        kacc[h, 256:512, :] = nn(w1, qh[h, 256:512, :])
        vacc[h, 0:256, :] = nt(probsT[h, 0:256, :], go)
        vacc[h, 256:512, :] = nt(probsT[h, 256:512, 256:], go[:, 256:])

    backward(0)
    backward(1)
    at = jnp.where(idx == 7, 0.0, idxf + 1.0)
    coefs = []
    for j in source:
        first_j = jnp.sum(jnp.where(idx == j, first_g, 0.0), axis=0, keepdims=True)
        jf = j.astype(f32)
        coefs.append(fade(rate_y, (jf >= at) & (first_j <= BLK * at), jf - at))
    u_copies = {}
    for c in range(CHUNKS):
        for d in (1, 3, 2):
            c_copies[d, c].wait()
        total_c = coefs[0][7:8, :] * bown[y, chunk(c), :]
        for d in range(1, GROUP):
            total_c = total_c + coefs[d][7:8, :] * brec[d, chunk(c), :]
        bsum[chunk(c), :] = total_c
        for n in (1, 0):
            u_copies[n, c] = remote(
                bsum.at[chunk(c)], bin_.at[n, chunk(c)], u_s.at[n, c], u_r.at[n, c], col_dev(-(n + 1))
            )
    for i in range(GROUP - 1):
        outer = coefs[0][i : i + 1, :] * bown[y]
        for d in range(1, GROUP):
            outer = outer + coefs[d][i : i + 1, :] * brec[d]
        bout[i] = outer
    backward(2)
    backward(3)
    oq[...] = so_q[...].astype(bf16)
    far = fade(rate_y, first_g <= BLK * GROUP, jnp.full((8, 128), GROUP, f32))[6:7, :]
    carry = fade(rate_y, first_g[4:5, :] <= BLK * (idxf + 1.0), GROUP - 1.0 - idxf)
    w_copies = {}
    for c in range(CHUNKS):
        for n in (0, 1):
            u_copies[n, c].wait()
        enter = bin_[0, chunk(c), :] + far * bin_[1, chunk(c), :]
        bout[GROUP - 1, chunk(c), :] = enter
        for i in range(GROUP - 1):
            bout[i, chunk(c), :] = bout[i, chunk(c), :] + carry[i : i + 1, :] * enter
        for d in (2, 1, 3):
            w_copies[d, c] = remote(
                bout.at[(y + d) % GROUP, chunk(c)], bent.at[y, chunk(c)], w_s.at[d, c], w_r.at[d, c], row_dev(d)
            )
    bent[y] = bout[y]

    for d in (0, 1, 3, 2):
        h = source[d]
        if d:
            for c in range(CHUNKS):
                w_copies[d, c].wait()
        state = bent[h].astype(bf16)
        so_k[pl.ds(h, BLK, stride=HPD), :] = kacc[h] + backc[h] * nt(vh[h], state)
        so_v[pl.ds(h, BLK, stride=HPD), :] = vacc[h] + backc[h] * nn(kh[h], state)
    ok[...] = so_k[...].astype(bf16)
    ov[...] = so_v[...].astype(bf16)


def copy_out(a, b, c, a_hbm, b_hbm, c_hbm, sems):
    copies = [
        pltpu.make_async_copy(s, t, sems.at[i])
        for i, (s, t) in enumerate(((a, a_hbm), (b, b_hbm), (c, c_hbm)))
    ]
    for x in copies:
        x.start()
    for x in copies:
        x.wait()


def local(zs, hs, queries, keys, values, out_grad, gain, decay_rate, doc_lengths):
    rows = BLK * HPD
    flat = [a.reshape(rows, FEAT) for a in (queries, keys, values, out_grad)]
    hbm = pl.BlockSpec(memory_space=pltpu.HBM)
    vmem = pl.BlockSpec(memory_space=pltpu.VMEM)
    V = pltpu.VMEM
    mat = (FEAT, FEAT)
    chain = [
        V((HPD,) + mat, f32), V((GROUP,) + mat, f32), V(mat, f32),
        V((2,) + mat, f32), V((GROUP,) + mat, f32), V((HPD,) + mat, f32),
    ]
    scratch = (
        [V((rows, FEAT), bf16)] * 4
        + [V((rows, FEAT), f32)] * 4
        + [V((HPD, BLK, FEAT), bf16)] * 3
        + [V((HPD, FEAT, BLK), bf16)] * 3
        + [V((HPD, FEAT, BLK), f32), V((BLK, BLK), f32), V((HPD, BLK, BLK), f32), V((HPD, BLK, BLK), bf16)]
        + [V((HPD, FEAT, BLK), f32), V((HPD, FEAT, BLK), bf16)]
        + chain + chain
        + [V((8, 128), f32), V((hs, 8, 128), f32)]
        + [V((HPD, BLK, FEAT), f32)] * 3
        + [V((rows, FEAT), f32)] * 3
        + [V((HPD, FEAT), f32), pltpu.SMEM((1, HPD), f32), V((1, doc_lengths.shape[0]), jnp.int32)]
    )
    dma = pltpu.SemaphoreType.DMA
    moves = [dma((GROUP, CHUNKS))] * 2 + [dma((2, CHUNKS))] * 2 + [dma((GROUP, CHUNKS))] * 2
    sems = [dma((7,))] + moves + [dma((hs,))] * 2 + moves
    operands = (*flat, gain, decay_rate.reshape(1, HPD), doc_lengths.reshape(1, doc_lengths.shape[0]))
    result = [jax.ShapeDtypeStruct((rows, FEAT), bf16)] * 3
    outs = pl.pallas_call(
        functools.partial(kernel, zs, hs, zs * GROUP * BLK, hs * HPD * FEAT),
        out_shape=[V((rows, FEAT), bf16)] * 3,
        in_specs=[hbm] * 7,
        out_specs=[vmem] * 3,
        scratch_shapes=scratch + sems,
        compiler_params=pltpu.CompilerParams(
            collective_id=0, has_side_effects=True, vmem_limit_bytes=40 * 2**20
        ),
        cost_estimate=pl.CostEstimate(flops=2 * 10**9, bytes_accessed=4 * 10**6, transcendentals=10**6),
    )(*(pltpu.with_memory_space_constraint(a, pltpu.HBM) for a in operands))
    outs = pl.pallas_call(
        copy_out, out_shape=result, in_specs=[vmem] * 3, out_specs=[hbm] * 3, scratch_shapes=[dma((3,))],
        compiler_params=pltpu.CompilerParams(vmem_limit_bytes=2**20),
    )(*outs)
    return tuple(o.reshape(BLK, HPD, FEAT) for o in outs)


def solution(mesh):
    spec = P("ctx", "head", None)
    zs, hs = mesh.shape["ctx"] // GROUP, mesh.shape["head"]
    return jax.shard_map(
        functools.partial(local, zs, hs), mesh=mesh,
        in_specs=(spec,) * 4 + (P("head", None), P("head"), P()),
        out_specs=(spec,) * 3, check_vma=False,
    )
```

```python
import functools

import jax
import jax.numpy as jnp
from jax import lax
from jax.experimental import pallas as pl
from jax.experimental.pallas import tpu as pltpu
from jax.sharding import PartitionSpec as P

epsilon = 1e-06
BLK = 512
GROUP = 4
FEAT = 128
HPD = 4
FAR = 1e37
f32 = jnp.float32
bf16 = jnp.bfloat16
PARTS = ((0, 256, 0), (256, 512, 256))
CHUNKS = 4
ROWS = FEAT // CHUNKS


def nn(a, b):
    return lax.dot_general(a, b, (((1,), (0,)), ((), ())), preferred_element_type=f32)


def nt(a, b):
    return lax.dot_general(a, b, (((1,), (1,)), ((), ())), preferred_element_type=f32)


def kernel(
    zs, hs, total, width,
    q_hbm, k_hbm, v_hbm, g_hbm, gain_hbm, rate_hbm, lens_hbm,
    oq, ok, ov,
    qin, kin, vin, gin, st_q, st_k, st_v, st_g,
    qh, kh, vh, qT, kT, vT, gT, dist, decay, probsT, oT, goT,
    fown, frec, fsum, fin, fout, fent,
    bown, brec, bsum, bin_, bout, bent,
    stat, stats, kacc, vacc, backc, so_q, so_k, so_v, gain_ref, rate_ref, lens_ref,
    in_sem, above, a_s, a_r, t_s, t_r, e_s, e_r, n_s, n_r, c_s, c_r, u_s, u_r, w_s, w_r,
):
    head = lax.axis_index("head")
    ctx = lax.axis_index("ctx")
    z = ctx // GROUP
    y = ctx % GROUP

    def row_dev(d):
        return {"ctx": z * GROUP + (y + d) % GROUP}

    def col_dev(d):
        return {"ctx": ((z + d + zs) % zs) * GROUP + y}

    def head_dev(m):
        return {"head": (head + m) % hs}

    def signal(semaphore, device):
        pl.semaphore_signal(semaphore, inc=1, device_id=device, device_id_type=pl.DeviceIdType.MESH)

    loads = [
        pltpu.make_async_copy(s, t, in_sem.at[i])
        for i, (s, t) in enumerate(
            (
                (k_hbm, kin), (v_hbm, vin), (lens_hbm, lens_ref), (rate_hbm, rate_ref),
                (q_hbm, qin), (g_hbm, gin), (gain_hbm, gain_ref),
            )
        )
    ]
    barrier = pltpu.get_barrier_semaphore()
    for d in (2, 1, 3):
        signal(barrier, row_dev(d))
    for c in loads[:4]:
        c.start()
    for n in (2, 1):
        @pl.when(z < zs - n)
        def _(n=n):
            signal(barrier, col_dev(n))
    for m in range(1, hs):
        signal(barrier, head_dev(m))
    for c in loads[4:]:
        c.start()

    def enter():
        for n, below in ((0, z == 0), (1, z == 1), (2, z > 1)):
            @pl.when(below)
            def _(n=n):
                pl.semaphore_wait(barrier, GROUP - 1 + hs - 1 + n)
        for n in (1, 2):
            @pl.when(z >= n)
            def _(n=n):
                signal(above, col_dev(-n))
            @pl.when(z < n)
            def _(n=n):
                fin[n - 1] = jnp.zeros((FEAT, FEAT), f32)
            @pl.when(z >= zs - n)
            def _(n=n):
                bin_[n - 1] = jnp.zeros((FEAT, FEAT), f32)

    sent = []

    def always(action):
        action()

    def remote(source, target, sends, receives, device, there=always, here=always):
        copy = pltpu.make_async_remote_copy(
            src_ref=source, dst_ref=target, send_sem=sends, recv_sem=receives,
            device_id=device, device_id_type=pl.DeviceIdType.MESH,
        )
        there(copy.start)
        sent.append((copy, there))
        return lambda: here(copy.wait_recv)

    def drain(copies):
        for copy, there in copies:
            there(copy.wait_send)

    def chunk(c):
        return pl.ds(c * ROWS, ROWS)

    def fade(rate, mask, count):
        return jnp.where(mask, jnp.exp(-rate * (BLK * jnp.maximum(count, 0.0))), 0.0)

    loads[2].wait()
    loads[3].wait()
    b0 = (ctx * BLK).astype(f32)
    g0 = (z * (BLK * GROUP)).astype(f32)
    lens = jnp.broadcast_to(lens_ref[...].astype(f32), (128, 128))
    low = lax.broadcasted_iota(jnp.int32, (128, 128), 0) < lax.broadcasted_iota(jnp.int32, (128, 128), 1)
    starts = jnp.sum(jnp.where(low, lens.T, 0.0), axis=0, keepdims=True)
    starts_c = jnp.broadcast_to(starts, (128, 128)).T
    t_row = lax.broadcasted_iota(jnp.int32, (1, BLK), 1).astype(f32)
    own_start = jnp.concatenate(
        [
            jnp.max(
                jnp.where(starts_c - b0 <= t_row[:, i : i + 128], starts_c - b0, -2.0 * total),
                axis=0, keepdims=True,
            )
            for i in range(0, BLK, 128)
        ],
        axis=1,
    )

    def start_of(position):
        found = jnp.max(jnp.where(starts <= position, starts, -1.0), axis=1, keepdims=True)
        found = jnp.broadcast_to(found, (8, 128))
        return jnp.where(position >= total, f32(total), found)

    idx = lax.broadcasted_iota(jnp.int32, (8, 128), 0)
    idxf = idx.astype(f32)
    ends = start_of(jnp.where(idx == 5, b0 + (BLK - 1.0), g0 + idxf * BLK - 1.0))
    firsts = start_of(jnp.where(idx == 5, b0 + BLK, jnp.where(idx == 6, g0 + 2.0 * BLK * GROUP, g0 + idxf * BLK)))
    end_g = ends - g0
    first_g = firsts - g0
    last_start = ends[5:6, 0:1] - b0
    next_start = firsts[5:6, :] - b0

    rate_y = rate_ref[0, y]
    in_mask = own_start < 0.0
    tail_mask = t_row >= last_start
    lead_mask = own_start <= 0.0

    def in_row(h):
        return jnp.where(in_mask, jnp.exp(-rate_ref[0, h] * (t_row + 1.0)), 0.0)

    def split_heads(source, stage):
        stage[...] = source[...].astype(f32)

    def of_head(stage, h):
        return stage[pl.ds(h, BLK, stride=HPD), :]

    loads[0].wait()
    split_heads(kin, st_k)
    loads[1].wait()
    split_heads(vin, st_v)
    a_copies = {}
    for d in (2, 1, 3, 0):
        h = (y + d) % GROUP
        k_f = of_head(st_k, h)
        k_t = k_f.T
        kh[h] = k_f.astype(bf16)
        kT[h] = k_t.astype(bf16)
        v_f = of_head(st_v, h)
        vh[h] = v_f.astype(bf16)
        tail = jnp.where(tail_mask, jnp.exp(-rate_ref[0, h] * (BLK - 1.0 - t_row)), 0.0)
        fown[h] = nn((k_t * tail).astype(bf16), v_f.astype(bf16))
        if not a_copies:
            enter()
        if d:
            for c in range(CHUNKS):
                a_copies[d, c] = remote(
                    fown.at[h, chunk(c)], frec.at[d, chunk(c)], a_s.at[d, c], a_r.at[d, c], row_dev(d)
                )

    loads[4].wait()
    split_heads(qin, st_q)
    loads[5].wait()
    split_heads(gin, st_g)
    loads[6].wait()
    gain_c = jnp.concatenate([gain_ref[...], jnp.zeros((FEAT - HPD, FEAT), f32)], axis=0).T

    s_col = lax.broadcasted_iota(jnp.int32, (BLK, BLK), 0).astype(f32)
    t_col = lax.broadcasted_iota(jnp.int32, (BLK, BLK), 1).astype(f32)
    dist[...] = jnp.where((s_col <= t_col) & (s_col >= own_start), t_col - s_col, FAR)

    def prepare(h):
        q_f = of_head(st_q, h)
        qh[h] = q_f.astype(bf16)
        qT[h] = q_f.T.astype(bf16)
        gT[h] = of_head(st_g, h).T * gain_c[:, h : h + 1]
        vT[h] = vh[h].astype(f32).T.astype(bf16)
        s_i = lax.broadcasted_iota(jnp.int32, (BLK, FEAT), 0).astype(f32)
        backc[h] = jnp.where(s_i >= next_start, jnp.exp(-rate_ref[0, h] * (BLK - s_i)), 0.0)

    def forward(h):
        prepare(h)
        for s0, s1, t0 in PARTS:
            w = jnp.exp(-rate_ref[0, h] * dist[s0:s1, t0:])
            decay[h, s0:s1, t0:] = w
            probsT[h, s0:s1, t0:] = (nn(kh[h, s0:s1, :], qT[h, :, t0:]) * w).astype(bf16)
        oT[h, :, 0:256] = nn(vT[h, :, 0:256], probsT[h, 0:256, 0:256])
        oT[h, :, 256:512] = nn(vT[h], probsT[h, :, 256:512])

    forward(0)
    forward(1)
    source = [(y + GROUP - d) % GROUP for d in range(GROUP)]
    coefs = [
        fade(
            rate_y, (idx > j) & (end_g <= BLK * (j.astype(f32) + 1.0) - 1.0), idxf - 1.0 - j.astype(f32)
        )
        for j in source
    ]
    for n, over in ((1, z == zs - 2), (2, z < zs - 2)):
        @pl.when(over)
        def _(n=n):
            pl.semaphore_wait(above, n)
    t_copies = {}
    for c in range(CHUNKS):
        for d in (1, 3, 2):
            a_copies[d, c]()
        total_c = coefs[0][GROUP : GROUP + 1, :] * fown[y, chunk(c), :]
        for d in range(1, GROUP):
            total_c = total_c + coefs[d][GROUP : GROUP + 1, :] * frec[d, chunk(c), :]
        fsum[chunk(c), :] = total_c
        for n in (1, 0):
            t_copies[n, c] = remote(
                fsum.at[chunk(c)], fin.at[n, chunk(c)], t_s.at[n, c], t_r.at[n, c], col_dev(n + 1),
                pl.when(z < zs - 1 - n), pl.when(z > n),
            )
    for i in range(1, GROUP):
        inner = coefs[0][i : i + 1, :] * fown[y]
        for d in range(1, GROUP):
            inner = inner + coefs[d][i : i + 1, :] * frec[d]
        fout[i] = inner
    forward(2)
    forward(3)
    far = fade(rate_y, end_g <= -BLK * GROUP - 1.0, jnp.full((8, 128), GROUP, f32))[0:1, :]
    carry = fade(rate_y, end_g <= -1.0, idxf)
    e_copies = {}
    for c in range(CHUNKS):
        for n in (0, 1):
            t_copies[n, c]()
        entry = fin[0, chunk(c), :] + far * fin[1, chunk(c), :]
        fout[0, chunk(c), :] = entry
        for i in range(1, GROUP):
            fout[i, chunk(c), :] = fout[i, chunk(c), :] + carry[i : i + 1, :] * entry
        for d in (2, 1, 3):
            e_copies[d, c] = remote(
                fout.at[(y + d) % GROUP, chunk(c)], fent.at[y, chunk(c)], e_s.at[d, c], e_r.at[d, c], row_dev(d)
            )
    fent[y] = fout[y]

    squares = jnp.zeros((8, BLK), f32)
    cross = jnp.zeros((8, BLK), f32)
    for d in (0, 1, 3, 2):
        h = source[d]
        if d:
            for c in range(CHUNKS):
                e_copies[d, c]()
        state = fent[h].T.astype(bf16)
        o = oT[h] + in_row(h) * nn(state, qT[h])
        oT[h] = o
        squares = squares + jnp.sum((o * o).reshape(FEAT // 8, 8, BLK), axis=0)
        cross = cross + jnp.sum((o * gT[h]).reshape(FEAT // 8, 8, BLK), axis=0)
    squares = jnp.sum(squares, axis=0, keepdims=True)
    cross = jnp.sum(cross, axis=0, keepdims=True)
    for i in range(4):
        stat[i : i + 1, :] = squares[:, i * 128 : (i + 1) * 128]
        stat[i + 4 : i + 5, :] = cross[:, i * 128 : (i + 1) * 128]
    n_copies = [
        remote(stat, stats.at[m], n_s.at[m], n_r.at[m], head_dev(m))
        for m in sorted(range(1, hs), key=lambda m: abs(m - hs // 2))
    ]
    for arrive in n_copies:
        arrive()
    both = stat[...]
    for m in range(1, hs):
        both = both + stats[m]
    inverse = 1.0 / jnp.sqrt(both[0:4, :] / width + epsilon)
    factor = both[4:8, :] * inverse * inverse * inverse / width
    inv_row = jnp.concatenate([inverse[i : i + 1, :] for i in range(4)], axis=1)
    fac_row = jnp.concatenate([factor[i : i + 1, :] for i in range(4)], axis=1)

    earlier = sent[:]
    sent.clear()
    c_copies = {}
    for d in (2, 1, 3, 0):
        h = (y + d) % GROUP
        go = (gT[h] * inv_row - oT[h] * fac_row).astype(bf16)
        goT[h] = go
        lead = jnp.where(lead_mask, jnp.exp(-rate_ref[0, h] * t_row), 0.0)
        bown[h] = nt((qT[h].astype(f32) * lead).astype(bf16), go)
        if d:
            for c in range(CHUNKS):
                c_copies[d, c] = remote(
                    bown.at[h, chunk(c)], brec.at[d, chunk(c)], c_s.at[d, c], c_r.at[d, c], row_dev(d)
                )

    def backward(h):
        go = goT[h]
        q_t = in_row(h) * nn(fent[h].astype(bf16), go)
        w0 = (nn(vh[h, 0:256, :], go) * decay[h, 0:256, :]).astype(bf16)
        w1 = (nn(vh[h, 256:512, :], go[:, 256:]) * decay[h, 256:512, 256:]).astype(bf16)
        q0 = q_t[:, 0:256] + nn(kT[h, :, 0:256], w0[:, 0:256])
        q1 = q_t[:, 256:] + nn(kT[h, :, 0:256], w0[:, 256:]) + nn(kT[h, :, 256:], w1)
        so_q[pl.ds(h, BLK, stride=HPD), :] = jnp.concatenate([q0.T, q1.T], axis=0)
        kacc[h, 0:256, :] = nn(w0, qh[h])
        kacc[h, 256:512, :] = nn(w1, qh[h, 256:512, :])
        vacc[h, 0:256, :] = nt(probsT[h, 0:256, :], go)
        vacc[h, 256:512, :] = nt(probsT[h, 256:512, 256:], go[:, 256:])

    drain(earlier)
    backward(0)
    backward(1)
    at = jnp.where(idx == 7, 0.0, idxf + 1.0)
    coefs = []
    for j in source:
        first_j = jnp.sum(jnp.where(idx == j, first_g, 0.0), axis=0, keepdims=True)
        jf = j.astype(f32)
        coefs.append(fade(rate_y, (jf >= at) & (first_j <= BLK * at), jf - at))
    u_copies = {}
    for c in range(CHUNKS):
        for d in (1, 3, 2):
            c_copies[d, c]()
        total_c = coefs[0][7:8, :] * bown[y, chunk(c), :]
        for d in range(1, GROUP):
            total_c = total_c + coefs[d][7:8, :] * brec[d, chunk(c), :]
        bsum[chunk(c), :] = total_c
        for n in (1, 0):
            u_copies[n, c] = remote(
                bsum.at[chunk(c)], bin_.at[n, chunk(c)], u_s.at[n, c], u_r.at[n, c], col_dev(-(n + 1)),
                pl.when(z > n), pl.when(z < zs - 1 - n),
            )
    for i in range(GROUP - 1):
        outer = coefs[0][i : i + 1, :] * bown[y]
        for d in range(1, GROUP):
            outer = outer + coefs[d][i : i + 1, :] * brec[d]
        bout[i] = outer
    backward(2)
    backward(3)
    oq[...] = so_q[...].astype(bf16)
    far = fade(rate_y, first_g <= BLK * GROUP, jnp.full((8, 128), GROUP, f32))[6:7, :]
    carry = fade(rate_y, first_g[4:5, :] <= BLK * (idxf + 1.0), GROUP - 1.0 - idxf)
    earlier = sent[:]
    sent.clear()
    w_copies = {}
    for c in range(CHUNKS):
        for n in (0, 1):
            u_copies[n, c]()
        entry = bin_[0, chunk(c), :] + far * bin_[1, chunk(c), :]
        bout[GROUP - 1, chunk(c), :] = entry
        for i in range(GROUP - 1):
            bout[i, chunk(c), :] = bout[i, chunk(c), :] + carry[i : i + 1, :] * entry
        for d in (2, 1, 3):
            w_copies[d, c] = remote(
                bout.at[(y + d) % GROUP, chunk(c)], bent.at[y, chunk(c)], w_s.at[d, c], w_r.at[d, c], row_dev(d)
            )
    bent[y] = bout[y]
    drain(earlier)

    for d in (0, 1, 3, 2):
        h = source[d]
        if d:
            for c in range(CHUNKS):
                w_copies[d, c]()
        state = bent[h].astype(bf16)
        so_k[pl.ds(h, BLK, stride=HPD), :] = kacc[h] + backc[h] * nt(vh[h], state)
        so_v[pl.ds(h, BLK, stride=HPD), :] = vacc[h] + backc[h] * nn(kh[h], state)
    drain(sent)
    ok[...] = so_k[...].astype(bf16)
    ov[...] = so_v[...].astype(bf16)


def copy_out(a, b, c, a_hbm, b_hbm, c_hbm, sems):
    copies = [
        pltpu.make_async_copy(s, t, sems.at[i])
        for i, (s, t) in enumerate(((a, a_hbm), (b, b_hbm), (c, c_hbm)))
    ]
    for x in copies:
        x.start()
    for x in copies:
        x.wait()


def local(zs, hs, queries, keys, values, out_grad, gain, decay_rate, doc_lengths):
    rows = BLK * HPD
    flat = [a.reshape(rows, FEAT) for a in (queries, keys, values, out_grad)]
    hbm = pl.BlockSpec(memory_space=pltpu.HBM)
    vmem = pl.BlockSpec(memory_space=pltpu.VMEM)
    V = pltpu.VMEM
    mat = (FEAT, FEAT)
    chain = [
        V((HPD,) + mat, f32), V((GROUP,) + mat, f32), V(mat, f32),
        V((2,) + mat, f32), V((GROUP,) + mat, f32), V((HPD,) + mat, f32),
    ]
    scratch = (
        [V((rows, FEAT), bf16)] * 4
        + [V((rows, FEAT), f32)] * 4
        + [V((HPD, BLK, FEAT), bf16)] * 3
        + [V((HPD, FEAT, BLK), bf16)] * 3
        + [V((HPD, FEAT, BLK), f32), V((BLK, BLK), f32), V((HPD, BLK, BLK), f32), V((HPD, BLK, BLK), bf16)]
        + [V((HPD, FEAT, BLK), f32), V((HPD, FEAT, BLK), bf16)]
        + chain + chain
        + [V((8, 128), f32), V((hs, 8, 128), f32)]
        + [V((HPD, BLK, FEAT), f32)] * 3
        + [V((rows, FEAT), f32)] * 3
        + [V((HPD, FEAT), f32), pltpu.SMEM((1, HPD), f32), V((1, doc_lengths.shape[0]), jnp.int32)]
    )
    dma = pltpu.SemaphoreType.DMA
    moves = [dma((GROUP, CHUNKS))] * 2 + [dma((2, CHUNKS))] * 2 + [dma((GROUP, CHUNKS))] * 2
    sems = [dma((7,)), pltpu.SemaphoreType.REGULAR] + moves + [dma((hs,))] * 2 + moves
    operands = (*flat, gain, decay_rate.reshape(1, HPD), doc_lengths.reshape(1, doc_lengths.shape[0]))
    result = [jax.ShapeDtypeStruct((rows, FEAT), bf16)] * 3
    outs = pl.pallas_call(
        functools.partial(kernel, zs, hs, zs * GROUP * BLK, hs * HPD * FEAT),
        out_shape=[V((rows, FEAT), bf16)] * 3,
        in_specs=[hbm] * 7,
        out_specs=[vmem] * 3,
        scratch_shapes=scratch + sems,
        compiler_params=pltpu.CompilerParams(
            collective_id=0, has_side_effects=True, vmem_limit_bytes=40 * 2**20
        ),
        cost_estimate=pl.CostEstimate(flops=2 * 10**9, bytes_accessed=4 * 10**6, transcendentals=10**6),
    )(*(pltpu.with_memory_space_constraint(a, pltpu.HBM) for a in operands))
    outs = pl.pallas_call(
        copy_out, out_shape=result, in_specs=[vmem] * 3, out_specs=[hbm] * 3, scratch_shapes=[dma((3,))],
        compiler_params=pltpu.CompilerParams(vmem_limit_bytes=2**20),
    )(*outs)
    return tuple(o.reshape(BLK, HPD, FEAT) for o in outs)


def solution(mesh):
    spec = P("ctx", "head", None)
    zs, hs = mesh.shape["ctx"] // GROUP, mesh.shape["head"]
    return jax.shard_map(
        functools.partial(local, zs, hs), mesh=mesh,
        in_specs=(spec,) * 4 + (P("head", None), P("head"), P()),
        out_specs=(spec,) * 3, check_vma=False,
    )
```

```python
import functools

import jax
import jax.numpy as jnp
from jax import lax
from jax.experimental import pallas as pl
from jax.experimental.pallas import tpu as pltpu
from jax.sharding import PartitionSpec as P

epsilon = 1e-06
BLK = 512
GROUP = 4
FEAT = 128
HPD = 4
FAR = 1e37
f32 = jnp.float32
bf16 = jnp.bfloat16
PARTS = ((0, 256, 0), (256, 512, 256))
CHUNKS = 4
ROWS = FEAT // CHUNKS


def nn(a, b):
    return lax.dot_general(a, b, (((1,), (0,)), ((), ())), preferred_element_type=f32)


def nt(a, b):
    return lax.dot_general(a, b, (((1,), (1,)), ((), ())), preferred_element_type=f32)


def kernel(
    zs, hs, total, width,
    q_hbm, k_hbm, v_hbm, g_hbm, gain_hbm, rate_hbm, lens_hbm,
    oq, ok, ov,
    qin, kin, vin, gin, st_q, st_k, st_v, st_g,
    qh, kh, vh, qT, kT, vT, gT, dist, decay, probsT, oT, goT,
    fown, frec, fsum, fin, fout, fent,
    bown, brec, bsum, bin_, bout, bent,
    stat, stats, kacc, vacc, backc, so_q, so_k, so_v, gain_ref, rate_ref, lens_ref,
    in_sem, above, a_s, a_r, t_s, t_r, e_s, e_r, n_s, n_r, c_s, c_r, u_s, u_r, w_s, w_r,
):
    head = lax.axis_index("head")
    ctx = lax.axis_index("ctx")
    z = ctx // GROUP
    y = ctx % GROUP

    def row_dev(d):
        return {"ctx": z * GROUP + (y + d) % GROUP}

    def col_dev(d):
        return {"ctx": ((z + d + zs) % zs) * GROUP + y}

    def head_dev(m):
        return {"head": (head + m) % hs}

    def signal(semaphore, device):
        pl.semaphore_signal(semaphore, inc=1, device_id=device, device_id_type=pl.DeviceIdType.MESH)

    loads = [
        pltpu.make_async_copy(s, t, in_sem.at[i])
        for i, (s, t) in enumerate(
            (
                (k_hbm, kin), (v_hbm, vin), (lens_hbm, lens_ref), (rate_hbm, rate_ref),
                (q_hbm, qin), (g_hbm, gin), (gain_hbm, gain_ref),
            )
        )
    ]
    barrier = pltpu.get_barrier_semaphore()
    for d in (2, 1, 3):
        signal(barrier, row_dev(d))
    for c in loads[:4]:
        c.start()
    for n in (2, 1):
        @pl.when(z < zs - n)
        def _(n=n):
            signal(barrier, col_dev(n))
    for m in range(1, hs):
        signal(barrier, head_dev(m))
    for c in loads[4:]:
        c.start()

    def enter():
        for n, below in ((0, z == 0), (1, z == 1), (2, z > 1)):
            @pl.when(below)
            def _(n=n):
                pl.semaphore_wait(barrier, GROUP - 1 + hs - 1 + n)
        for n in (1, 2):
            @pl.when(z >= n)
            def _(n=n):
                signal(above, col_dev(-n))
            @pl.when(z < n)
            def _(n=n):
                fin[n - 1] = jnp.zeros((FEAT, FEAT), f32)
            @pl.when(z >= zs - n)
            def _(n=n):
                bin_[n - 1] = jnp.zeros((FEAT, FEAT), f32)

    sent = []

    def always(action):
        action()

    def remote(source, target, sends, receives, device, there=always, here=always):
        copy = pltpu.make_async_remote_copy(
            src_ref=source, dst_ref=target, send_sem=sends, recv_sem=receives,
            device_id=device, device_id_type=pl.DeviceIdType.MESH,
        )
        there(copy.start)
        sent.append((copy, there))
        return lambda: here(copy.wait_recv)

    def drain(copies):
        for copy, there in copies:
            there(copy.wait_send)

    def chunk(c):
        return pl.ds(c * ROWS, ROWS)

    def fade(rate, mask, count):
        return jnp.where(mask, jnp.exp(-rate * (BLK * jnp.maximum(count, 0.0))), 0.0)

    loads[2].wait()
    loads[3].wait()
    b0 = (ctx * BLK).astype(f32)
    g0 = (z * (BLK * GROUP)).astype(f32)
    lens = jnp.broadcast_to(lens_ref[...].astype(f32), (128, 128))
    low = lax.broadcasted_iota(jnp.int32, (128, 128), 0) < lax.broadcasted_iota(jnp.int32, (128, 128), 1)
    starts = jnp.sum(jnp.where(low, lens.T, 0.0), axis=0, keepdims=True)
    starts_c = jnp.broadcast_to(starts, (128, 128)).T
    t_row = lax.broadcasted_iota(jnp.int32, (1, BLK), 1).astype(f32)
    own_start = jnp.concatenate(
        [
            jnp.max(
                jnp.where(starts_c - b0 <= t_row[:, i : i + 128], starts_c - b0, -2.0 * total),
                axis=0, keepdims=True,
            )
            for i in range(0, BLK, 128)
        ],
        axis=1,
    )

    def start_of(position):
        found = jnp.max(jnp.where(starts <= position, starts, -1.0), axis=1, keepdims=True)
        found = jnp.broadcast_to(found, (8, 128))
        return jnp.where(position >= total, f32(total), found)

    idx = lax.broadcasted_iota(jnp.int32, (8, 128), 0)
    idxf = idx.astype(f32)
    ends = start_of(jnp.where(idx == 5, b0 + (BLK - 1.0), g0 + idxf * BLK - 1.0))
    firsts = start_of(jnp.where(idx == 5, b0 + BLK, jnp.where(idx == 6, g0 + 2.0 * BLK * GROUP, g0 + idxf * BLK)))
    end_g = ends - g0
    first_g = firsts - g0
    last_start = ends[5:6, 0:1] - b0
    next_start = firsts[5:6, :] - b0

    rate_y = rate_ref[0, y]
    in_mask = own_start < 0.0
    tail_mask = t_row >= last_start
    lead_mask = own_start <= 0.0

    def in_row(h):
        return jnp.where(in_mask, jnp.exp(-rate_ref[0, h] * (t_row + 1.0)), 0.0)

    def split_heads(source, stage):
        stage[...] = source[...].astype(f32)

    def of_head(stage, h):
        return stage[pl.ds(h, BLK, stride=HPD), :]

    loads[0].wait()
    split_heads(kin, st_k)
    loads[1].wait()
    split_heads(vin, st_v)
    a_copies = {}
    for d in (2, 1, 3, 0):
        h = (y + d) % GROUP
        k_f = of_head(st_k, h)
        k_t = k_f.T
        kh[h] = k_f.astype(bf16)
        kT[h] = k_t.astype(bf16)
        v_f = of_head(st_v, h)
        vh[h] = v_f.astype(bf16)
        tail = jnp.where(tail_mask, jnp.exp(-rate_ref[0, h] * (BLK - 1.0 - t_row)), 0.0)
        fown[h] = nn((k_t * tail).astype(bf16), v_f.astype(bf16))
        if not a_copies:
            enter()
        if d:
            for c in range(CHUNKS):
                a_copies[d, c] = remote(
                    fown.at[h, chunk(c)], frec.at[d, chunk(c)], a_s.at[d, c], a_r.at[d, c], row_dev(d)
                )

    loads[4].wait()
    split_heads(qin, st_q)
    loads[5].wait()
    split_heads(gin, st_g)
    loads[6].wait()
    gain_c = jnp.concatenate([gain_ref[...], jnp.zeros((FEAT - HPD, FEAT), f32)], axis=0).T

    s_col = lax.broadcasted_iota(jnp.int32, (BLK, BLK), 0).astype(f32)
    t_col = lax.broadcasted_iota(jnp.int32, (BLK, BLK), 1).astype(f32)
    dist[...] = jnp.where((s_col <= t_col) & (s_col >= own_start), t_col - s_col, FAR)

    def prepare(h):
        q_f = of_head(st_q, h)
        qh[h] = q_f.astype(bf16)
        qT[h] = q_f.T.astype(bf16)
        gT[h] = of_head(st_g, h).T * gain_c[:, h : h + 1]
        vT[h] = vh[h].astype(f32).T.astype(bf16)
        s_i = lax.broadcasted_iota(jnp.int32, (BLK, FEAT), 0).astype(f32)
        backc[h] = jnp.where(s_i >= next_start, jnp.exp(-rate_ref[0, h] * (BLK - s_i)), 0.0)

    def forward(h):
        prepare(h)
        for s0, s1, t0 in PARTS:
            w = jnp.exp(-rate_ref[0, h] * dist[s0:s1, t0:])
            decay[h, s0:s1, t0:] = w
            probsT[h, s0:s1, t0:] = (nn(kh[h, s0:s1, :], qT[h, :, t0:]) * w).astype(bf16)
        oT[h, :, 0:256] = nn(vT[h, :, 0:256], probsT[h, 0:256, 0:256])
        oT[h, :, 256:512] = nn(vT[h], probsT[h, :, 256:512])

    forward(0)
    forward(1)
    source = [(y + GROUP - d) % GROUP for d in range(GROUP)]
    coefs = [
        fade(
            rate_y, (idx > j) & (end_g <= BLK * (j.astype(f32) + 1.0) - 1.0), idxf - 1.0 - j.astype(f32)
        )
        for j in source
    ]
    for n, over in ((1, z == zs - 2), (2, z < zs - 2)):
        @pl.when(over)
        def _(n=n):
            pl.semaphore_wait(above, n)
    t_copies = {}
    for c in range(CHUNKS):
        for d in (1, 3, 2):
            a_copies[d, c]()
        total_c = coefs[0][GROUP : GROUP + 1, :] * fown[y, chunk(c), :]
        for d in range(1, GROUP):
            total_c = total_c + coefs[d][GROUP : GROUP + 1, :] * frec[d, chunk(c), :]
        fsum[chunk(c), :] = total_c
        for n in (1, 0):
            t_copies[n, c] = remote(
                fsum.at[chunk(c)], fin.at[n, chunk(c)], t_s.at[n, c], t_r.at[n, c], col_dev(n + 1),
                pl.when(z < zs - 1 - n), pl.when(z > n),
            )
    for i in range(1, GROUP):
        inner = coefs[0][i : i + 1, :] * fown[y]
        for d in range(1, GROUP):
            inner = inner + coefs[d][i : i + 1, :] * frec[d]
        fout[i] = inner
    forward(2)
    forward(3)
    far = fade(rate_y, end_g <= -BLK * GROUP - 1.0, jnp.full((8, 128), GROUP, f32))[0:1, :]
    carry = fade(rate_y, end_g <= -1.0, idxf)
    e_copies = {}
    for c in range(CHUNKS):
        for n in (0, 1):
            t_copies[n, c]()
        entry = fin[0, chunk(c), :] + far * fin[1, chunk(c), :]
        fout[0, chunk(c), :] = entry
        for i in range(1, GROUP):
            fout[i, chunk(c), :] = fout[i, chunk(c), :] + carry[i : i + 1, :] * entry
        for d in (2, 1, 3):
            e_copies[d, c] = remote(
                fout.at[(y + d) % GROUP, chunk(c)], fent.at[y, chunk(c)], e_s.at[d, c], e_r.at[d, c], row_dev(d)
            )
    fent[y] = fout[y]

    squares = jnp.zeros((8, BLK), f32)
    cross = jnp.zeros((8, BLK), f32)
    for d in (0, 1, 3, 2):
        h = source[d]
        if d:
            for c in range(CHUNKS):
                e_copies[d, c]()
        state = fent[h].T.astype(bf16)
        o = oT[h] + in_row(h) * nn(state, qT[h])
        oT[h] = o
        squares = squares + jnp.sum((o * o).reshape(FEAT // 8, 8, BLK), axis=0)
        cross = cross + jnp.sum((o * gT[h]).reshape(FEAT // 8, 8, BLK), axis=0)
    squares = jnp.sum(squares, axis=0, keepdims=True)
    cross = jnp.sum(cross, axis=0, keepdims=True)
    for i in range(4):
        stat[i : i + 1, :] = squares[:, i * 128 : (i + 1) * 128]
        stat[i + 4 : i + 5, :] = cross[:, i * 128 : (i + 1) * 128]
    n_copies = [
        remote(stat, stats.at[m], n_s.at[m], n_r.at[m], head_dev(m))
        for m in sorted(range(1, hs), key=lambda m: abs(m - hs // 2))
    ]
    for arrive in n_copies:
        arrive()
    both = stat[...]
    for m in range(1, hs):
        both = both + stats[m]
    inverse = 1.0 / jnp.sqrt(both[0:4, :] / width + epsilon)
    factor = both[4:8, :] * inverse * inverse * inverse / width
    inv_row = jnp.concatenate([inverse[i : i + 1, :] for i in range(4)], axis=1)
    fac_row = jnp.concatenate([factor[i : i + 1, :] for i in range(4)], axis=1)

    def gradient_state(h):
        go = (gT[h] * inv_row - oT[h] * fac_row).astype(bf16)
        goT[h] = go
        lead = jnp.where(lead_mask, jnp.exp(-rate_ref[0, h] * t_row), 0.0)
        bown[h] = nt((qT[h].astype(f32) * lead).astype(bf16), go)

    for d in (2, 1, 3):
        gradient_state((y + d) % GROUP)
    earlier = sent[:]
    sent.clear()
    c_copies = {}
    for c in range(CHUNKS):
        for d in (2, 1, 3):
            h = (y + d) % GROUP
            c_copies[d, c] = remote(
                bown.at[h, chunk(c)], brec.at[d, chunk(c)], c_s.at[d, c], c_r.at[d, c], row_dev(d)
            )
    gradient_state(y)

    def backward(h):
        go = goT[h]
        q_t = in_row(h) * nn(fent[h].astype(bf16), go)
        w0 = (nn(vh[h, 0:256, :], go) * decay[h, 0:256, :]).astype(bf16)
        w1 = (nn(vh[h, 256:512, :], go[:, 256:]) * decay[h, 256:512, 256:]).astype(bf16)
        q0 = q_t[:, 0:256] + nn(kT[h, :, 0:256], w0[:, 0:256])
        q1 = q_t[:, 256:] + nn(kT[h, :, 0:256], w0[:, 256:]) + nn(kT[h, :, 256:], w1)
        so_q[pl.ds(h, BLK, stride=HPD), :] = jnp.concatenate([q0.T, q1.T], axis=0)
        kacc[h, 0:256, :] = nn(w0, qh[h])
        kacc[h, 256:512, :] = nn(w1, qh[h, 256:512, :])
        vacc[h, 0:256, :] = nt(probsT[h, 0:256, :], go)
        vacc[h, 256:512, :] = nt(probsT[h, 256:512, 256:], go[:, 256:])

    drain(earlier)
    backward(0)
    backward(1)
    at = jnp.where(idx == 7, 0.0, idxf + 1.0)
    coefs = []
    for j in source:
        first_j = jnp.sum(jnp.where(idx == j, first_g, 0.0), axis=0, keepdims=True)
        jf = j.astype(f32)
        coefs.append(fade(rate_y, (jf >= at) & (first_j <= BLK * at), jf - at))
    u_copies = {}
    for c in range(CHUNKS):
        for d in (1, 3, 2):
            c_copies[d, c]()
        total_c = coefs[0][7:8, :] * bown[y, chunk(c), :]
        for d in range(1, GROUP):
            total_c = total_c + coefs[d][7:8, :] * brec[d, chunk(c), :]
        bsum[chunk(c), :] = total_c
        for n in (1, 0):
            u_copies[n, c] = remote(
                bsum.at[chunk(c)], bin_.at[n, chunk(c)], u_s.at[n, c], u_r.at[n, c], col_dev(-(n + 1)),
                pl.when(z > n), pl.when(z < zs - 1 - n),
            )
    for i in range(GROUP - 1):
        outer = coefs[0][i : i + 1, :] * bown[y]
        for d in range(1, GROUP):
            outer = outer + coefs[d][i : i + 1, :] * brec[d]
        bout[i] = outer
    backward(2)
    backward(3)
    oq[...] = so_q[...].astype(bf16)
    far = fade(rate_y, first_g <= BLK * GROUP, jnp.full((8, 128), GROUP, f32))[6:7, :]
    carry = fade(rate_y, first_g[4:5, :] <= BLK * (idxf + 1.0), GROUP - 1.0 - idxf)
    earlier = sent[:]
    sent.clear()
    w_copies = {}
    for c in range(CHUNKS):
        for n in (0, 1):
            u_copies[n, c]()
        entry = bin_[0, chunk(c), :] + far * bin_[1, chunk(c), :]
        bout[GROUP - 1, chunk(c), :] = entry
        for i in range(GROUP - 1):
            bout[i, chunk(c), :] = bout[i, chunk(c), :] + carry[i : i + 1, :] * entry
        for d in (2, 1, 3):
            w_copies[d, c] = remote(
                bout.at[(y + d) % GROUP, chunk(c)], bent.at[y, chunk(c)], w_s.at[d, c], w_r.at[d, c], row_dev(d)
            )
    bent[y] = bout[y]
    drain(earlier)

    for d in (0, 1, 3, 2):
        h = source[d]
        if d:
            for c in range(CHUNKS):
                w_copies[d, c]()
        state = bent[h].astype(bf16)
        so_k[pl.ds(h, BLK, stride=HPD), :] = kacc[h] + backc[h] * nt(vh[h], state)
        so_v[pl.ds(h, BLK, stride=HPD), :] = vacc[h] + backc[h] * nn(kh[h], state)
    drain(sent)
    ok[...] = so_k[...].astype(bf16)
    ov[...] = so_v[...].astype(bf16)


def copy_out(a, b, c, a_hbm, b_hbm, c_hbm, sems):
    copies = [
        pltpu.make_async_copy(s, t, sems.at[i])
        for i, (s, t) in enumerate(((a, a_hbm), (b, b_hbm), (c, c_hbm)))
    ]
    for x in copies:
        x.start()
    for x in copies:
        x.wait()


def local(zs, hs, queries, keys, values, out_grad, gain, decay_rate, doc_lengths):
    rows = BLK * HPD
    flat = [a.reshape(rows, FEAT) for a in (queries, keys, values, out_grad)]
    hbm = pl.BlockSpec(memory_space=pltpu.HBM)
    vmem = pl.BlockSpec(memory_space=pltpu.VMEM)
    V = pltpu.VMEM
    mat = (FEAT, FEAT)
    chain = [
        V((HPD,) + mat, f32), V((GROUP,) + mat, f32), V(mat, f32),
        V((2,) + mat, f32), V((GROUP,) + mat, f32), V((HPD,) + mat, f32),
    ]
    scratch = (
        [V((rows, FEAT), bf16)] * 4
        + [V((rows, FEAT), f32)] * 4
        + [V((HPD, BLK, FEAT), bf16)] * 3
        + [V((HPD, FEAT, BLK), bf16)] * 3
        + [V((HPD, FEAT, BLK), f32), V((BLK, BLK), f32), V((HPD, BLK, BLK), f32), V((HPD, BLK, BLK), bf16)]
        + [V((HPD, FEAT, BLK), f32), V((HPD, FEAT, BLK), bf16)]
        + chain + chain
        + [V((8, 128), f32), V((hs, 8, 128), f32)]
        + [V((HPD, BLK, FEAT), f32)] * 3
        + [V((rows, FEAT), f32)] * 3
        + [V((HPD, FEAT), f32), pltpu.SMEM((1, HPD), f32), V((1, doc_lengths.shape[0]), jnp.int32)]
    )
    dma = pltpu.SemaphoreType.DMA
    moves = [dma((GROUP, CHUNKS))] * 2 + [dma((2, CHUNKS))] * 2 + [dma((GROUP, CHUNKS))] * 2
    sems = [dma((7,)), pltpu.SemaphoreType.REGULAR] + moves + [dma((hs,))] * 2 + moves
    operands = (*flat, gain, decay_rate.reshape(1, HPD), doc_lengths.reshape(1, doc_lengths.shape[0]))
    result = [jax.ShapeDtypeStruct((rows, FEAT), bf16)] * 3
    outs = pl.pallas_call(
        functools.partial(kernel, zs, hs, zs * GROUP * BLK, hs * HPD * FEAT),
        out_shape=[V((rows, FEAT), bf16)] * 3,
        in_specs=[hbm] * 7,
        out_specs=[vmem] * 3,
        scratch_shapes=scratch + sems,
        compiler_params=pltpu.CompilerParams(
            collective_id=0, has_side_effects=True, vmem_limit_bytes=40 * 2**20
        ),
        cost_estimate=pl.CostEstimate(flops=2 * 10**9, bytes_accessed=4 * 10**6, transcendentals=10**6),
    )(*(pltpu.with_memory_space_constraint(a, pltpu.HBM) for a in operands))
    outs = pl.pallas_call(
        copy_out, out_shape=result, in_specs=[vmem] * 3, out_specs=[hbm] * 3, scratch_shapes=[dma((3,))],
        compiler_params=pltpu.CompilerParams(vmem_limit_bytes=2**20),
    )(*outs)
    return tuple(o.reshape(BLK, HPD, FEAT) for o in outs)


def solution(mesh):
    spec = P("ctx", "head", None)
    zs, hs = mesh.shape["ctx"] // GROUP, mesh.shape["head"]
    return jax.shard_map(
        functools.partial(local, zs, hs), mesh=mesh,
        in_specs=(spec,) * 4 + (P("head", None), P("head"), P()),
        out_specs=(spec,) * 3, check_vma=False,
    )
```

```python
import functools

import jax
import jax.numpy as jnp
from jax import lax
from jax.experimental import pallas as pl
from jax.experimental.pallas import tpu as pltpu
from jax.sharding import PartitionSpec as P

epsilon = 1e-06
BLK = 512
GROUP = 4
FEAT = 128
HPD = 4
FAR = 1e37
f32 = jnp.float32
bf16 = jnp.bfloat16
PARTS = ((0, 256, 0), (256, 512, 256))
CHUNKS = 4
ROWS = FEAT // CHUNKS


def nn(a, b):
    return lax.dot_general(a, b, (((1,), (0,)), ((), ())), preferred_element_type=f32)


def nt(a, b):
    return lax.dot_general(a, b, (((1,), (1,)), ((), ())), preferred_element_type=f32)


def kernel(
    zs, hs, total, width,
    q_hbm, k_hbm, v_hbm, g_hbm, gain_hbm, rate_hbm, lens_hbm,
    oq, ok, ov,
    qin, kin, vin, gin, st_q, st_k, st_v, st_g,
    qh, kh, vh, qT, kT, vT, gT, dist, decay, probsT, oT, goT,
    fown, frec, fsum, fin, fout, fent,
    bown, brec, bsum, bin_, bout, bent,
    stat, stats, kacc, vacc, backc, so_q, so_k, so_v, gain_ref, rate_ref, lens_ref,
    in_sem, above, a_s, a_r, t_s, t_r, e_s, e_r, n_s, n_r, c_s, c_r, u_s, u_r, w_s, w_r,
):
    head = lax.axis_index("head")
    ctx = lax.axis_index("ctx")
    z = ctx // GROUP
    y = ctx % GROUP

    def row_dev(d):
        return {"ctx": z * GROUP + (y + d) % GROUP}

    def col_dev(d):
        return {"ctx": ((z + d + zs) % zs) * GROUP + y}

    def head_dev(m):
        return {"head": (head + m) % hs}

    def signal(semaphore, device):
        pl.semaphore_signal(semaphore, inc=1, device_id=device, device_id_type=pl.DeviceIdType.MESH)

    loads = [
        pltpu.make_async_copy(s, t, in_sem.at[i])
        for i, (s, t) in enumerate(
            (
                (k_hbm, kin), (v_hbm, vin), (lens_hbm, lens_ref), (rate_hbm, rate_ref),
                (q_hbm, qin), (g_hbm, gin), (gain_hbm, gain_ref),
            )
        )
    ]
    barrier = pltpu.get_barrier_semaphore()
    for d in (2, 1, 3):
        signal(barrier, row_dev(d))
    for c in loads[:4]:
        c.start()
    for n in (2, 1):
        @pl.when(z < zs - n)
        def _(n=n):
            signal(barrier, col_dev(n))
    for m in range(1, hs):
        signal(barrier, head_dev(m))
    for c in loads[4:]:
        c.start()

    def enter():
        for n, below in ((0, z == 0), (1, z == 1), (2, z > 1)):
            @pl.when(below)
            def _(n=n):
                pl.semaphore_wait(barrier, GROUP - 1 + hs - 1 + n)
        for n in (1, 2):
            @pl.when(z >= n)
            def _(n=n):
                signal(above, col_dev(-n))
            @pl.when(z < n)
            def _(n=n):
                fin[n - 1] = jnp.zeros((FEAT, FEAT), f32)
            @pl.when(z >= zs - n)
            def _(n=n):
                bin_[n - 1] = jnp.zeros((FEAT, FEAT), f32)

    sent = []

    def always(action):
        action()

    def remote(source, target, sends, receives, device, there=always, here=always):
        copy = pltpu.make_async_remote_copy(
            src_ref=source, dst_ref=target, send_sem=sends, recv_sem=receives,
            device_id=device, device_id_type=pl.DeviceIdType.MESH,
        )
        there(copy.start)
        sent.append((copy, there))
        return lambda: here(copy.wait_recv)

    def drain(copies):
        for copy, there in copies:
            there(copy.wait_send)

    def chunk(c):
        return pl.ds(c * ROWS, ROWS)

    def fade(rate, mask, count):
        return jnp.where(mask, jnp.exp(-rate * (BLK * jnp.maximum(count, 0.0))), 0.0)

    loads[2].wait()
    loads[3].wait()
    b0 = (ctx * BLK).astype(f32)
    g0 = (z * (BLK * GROUP)).astype(f32)
    lens = jnp.broadcast_to(lens_ref[...].astype(f32), (128, 128))
    low = lax.broadcasted_iota(jnp.int32, (128, 128), 0) < lax.broadcasted_iota(jnp.int32, (128, 128), 1)
    starts = jnp.sum(jnp.where(low, lens.T, 0.0), axis=0, keepdims=True)
    starts_c = jnp.broadcast_to(starts, (128, 128)).T
    t_row = lax.broadcasted_iota(jnp.int32, (1, BLK), 1).astype(f32)
    own_start = jnp.concatenate(
        [
            jnp.max(
                jnp.where(starts_c - b0 <= t_row[:, i : i + 128], starts_c - b0, -2.0 * total),
                axis=0, keepdims=True,
            )
            for i in range(0, BLK, 128)
        ],
        axis=1,
    )

    def start_of(position):
        found = jnp.max(jnp.where(starts <= position, starts, -1.0), axis=1, keepdims=True)
        found = jnp.broadcast_to(found, (8, 128))
        return jnp.where(position >= total, f32(total), found)

    idx = lax.broadcasted_iota(jnp.int32, (8, 128), 0)
    idxf = idx.astype(f32)
    ends = start_of(jnp.where(idx == 5, b0 + (BLK - 1.0), g0 + idxf * BLK - 1.0))
    firsts = start_of(jnp.where(idx == 5, b0 + BLK, jnp.where(idx == 6, g0 + 2.0 * BLK * GROUP, g0 + idxf * BLK)))
    end_g = ends - g0
    first_g = firsts - g0
    last_start = ends[5:6, 0:1] - b0
    next_start = firsts[5:6, :] - b0

    rate_y = rate_ref[0, y]
    in_mask = own_start < 0.0
    tail_mask = t_row >= last_start
    lead_mask = own_start <= 0.0

    def in_row(h):
        return jnp.where(in_mask, jnp.exp(-rate_ref[0, h] * (t_row + 1.0)), 0.0)

    def split_heads(source, stage):
        stage[0 : BLK * HPD, :] = source[...].astype(f32)

    def of_head(stage, h):
        return stage[pl.ds(h, BLK, stride=HPD), :]

    loads[0].wait()
    split_heads(kin, st_k)
    loads[1].wait()
    split_heads(vin, st_v)
    a_copies = {}
    for d in (2, 1, 3, 0):
        h = (y + d) % GROUP
        k_f = of_head(st_k, h)
        k_t = k_f.T
        kh[h] = k_f.astype(bf16)
        kT[h] = k_t.astype(bf16)
        v_f = of_head(st_v, h)
        vh[h] = v_f.astype(bf16)
        tail = jnp.where(tail_mask, jnp.exp(-rate_ref[0, h] * (BLK - 1.0 - t_row)), 0.0)
        fown[h] = nn((k_t * tail).astype(bf16), v_f.astype(bf16))
        if not a_copies:
            enter()
        if d:
            for c in range(CHUNKS):
                a_copies[d, c] = remote(
                    fown.at[h, chunk(c)], frec.at[d, chunk(c)], a_s.at[d, c], a_r.at[d, c], row_dev(d)
                )

    loads[4].wait()
    split_heads(qin, st_q)
    loads[5].wait()
    split_heads(gin, st_g)
    loads[6].wait()
    gain_c = jnp.concatenate([gain_ref[...], jnp.zeros((FEAT - HPD, FEAT), f32)], axis=0).T

    s_col = lax.broadcasted_iota(jnp.int32, (BLK, BLK), 0).astype(f32)
    t_col = lax.broadcasted_iota(jnp.int32, (BLK, BLK), 1).astype(f32)
    dist[...] = jnp.where((s_col <= t_col) & (s_col >= own_start), t_col - s_col, FAR)

    def prepare(h):
        q_f = of_head(st_q, h)
        qh[h] = q_f.astype(bf16)
        qT[h] = q_f.T.astype(bf16)
        gT[h] = of_head(st_g, h).T * gain_c[:, h : h + 1]
        vT[h] = vh[h].astype(f32).T.astype(bf16)
        s_i = lax.broadcasted_iota(jnp.int32, (BLK, FEAT), 0).astype(f32)
        backc[h] = jnp.where(s_i >= next_start, jnp.exp(-rate_ref[0, h] * (BLK - s_i)), 0.0)

    def forward(h):
        prepare(h)
        for s0, s1, t0 in PARTS:
            w = jnp.exp(-rate_ref[0, h] * dist[s0:s1, t0:])
            decay[h, s0:s1, t0:] = w
            probsT[h, s0:s1, t0:] = (nn(kh[h, s0:s1, :], qT[h, :, t0:]) * w).astype(bf16)
        oT[h, :, 0:256] = nn(vT[h, :, 0:256], probsT[h, 0:256, 0:256])
        oT[h, :, 256:512] = nn(vT[h], probsT[h, :, 256:512])

    forward(0)
    forward(1)
    source = [(y + GROUP - d) % GROUP for d in range(GROUP)]
    coefs = [
        fade(
            rate_y, (idx > j) & (end_g <= BLK * (j.astype(f32) + 1.0) - 1.0), idxf - 1.0 - j.astype(f32)
        )
        for j in source
    ]
    for n, over in ((1, z == zs - 2), (2, z < zs - 2)):
        @pl.when(over)
        def _(n=n):
            pl.semaphore_wait(above, n)
    t_copies = {}
    for c in range(CHUNKS):
        for d in (1, 3, 2):
            a_copies[d, c]()
        total_c = coefs[0][GROUP : GROUP + 1, :] * fown[y, chunk(c), :]
        for d in range(1, GROUP):
            total_c = total_c + coefs[d][GROUP : GROUP + 1, :] * frec[d, chunk(c), :]
        fsum[chunk(c), :] = total_c
        for n in (1, 0):
            t_copies[n, c] = remote(
                fsum.at[chunk(c)], fin.at[n, chunk(c)], t_s.at[n, c], t_r.at[n, c], col_dev(n + 1),
                pl.when(z < zs - 1 - n), pl.when(z > n),
            )
    for i in range(1, GROUP):
        inner = coefs[0][i : i + 1, :] * fown[y]
        for d in range(1, GROUP):
            inner = inner + coefs[d][i : i + 1, :] * frec[d]
        fout[i] = inner
    forward(2)
    forward(3)
    far = fade(rate_y, end_g <= -BLK * GROUP - 1.0, jnp.full((8, 128), GROUP, f32))[0:1, :]
    carry = fade(rate_y, end_g <= -1.0, idxf)
    e_copies = {}
    for c in range(CHUNKS):
        for n in (0, 1):
            t_copies[n, c]()
        entry = fin[0, chunk(c), :] + far * fin[1, chunk(c), :]
        fout[0, chunk(c), :] = entry
        for i in range(1, GROUP):
            fout[i, chunk(c), :] = fout[i, chunk(c), :] + carry[i : i + 1, :] * entry
        for d in (2, 1, 3):
            e_copies[d, c] = remote(
                fout.at[(y + d) % GROUP, chunk(c)], fent.at[y, chunk(c)], e_s.at[d, c], e_r.at[d, c], row_dev(d)
            )
    fent[y] = fout[y]

    squares = jnp.zeros((8, BLK), f32)
    cross = jnp.zeros((8, BLK), f32)
    for d in (0, 1, 3, 2):
        h = source[d]
        if d:
            for c in range(CHUNKS):
                e_copies[d, c]()
        state = fent[h].T.astype(bf16)
        o = oT[h] + in_row(h) * nn(state, qT[h])
        oT[h] = o
        squares = squares + jnp.sum((o * o).reshape(FEAT // 8, 8, BLK), axis=0)
        cross = cross + jnp.sum((o * gT[h]).reshape(FEAT // 8, 8, BLK), axis=0)
    squares = jnp.sum(squares, axis=0, keepdims=True)
    cross = jnp.sum(cross, axis=0, keepdims=True)
    for i in range(4):
        stat[i : i + 1, :] = squares[:, i * 128 : (i + 1) * 128]
        stat[i + 4 : i + 5, :] = cross[:, i * 128 : (i + 1) * 128]
    n_copies = [
        remote(stat, stats.at[m], n_s.at[m], n_r.at[m], head_dev(m))
        for m in sorted(range(1, hs), key=lambda m: abs(m - hs // 2))
    ]
    for arrive in n_copies:
        arrive()
    both = stat[...]
    for m in range(1, hs):
        both = both + stats[m]
    inverse = 1.0 / jnp.sqrt(both[0:4, :] / width + epsilon)
    factor = both[4:8, :] * inverse * inverse * inverse / width
    inv_row = jnp.concatenate([inverse[i : i + 1, :] for i in range(4)], axis=1)
    fac_row = jnp.concatenate([factor[i : i + 1, :] for i in range(4)], axis=1)

    def gradient_state(h):
        go = (gT[h] * inv_row - oT[h] * fac_row).astype(bf16)
        goT[h] = go
        lead = jnp.where(lead_mask, jnp.exp(-rate_ref[0, h] * t_row), 0.0)
        bown[h] = nt((qT[h].astype(f32) * lead).astype(bf16), go)

    for d in (2, 1, 3):
        gradient_state((y + d) % GROUP)
    earlier = sent[:]
    sent.clear()
    c_copies = {}
    for c in range(CHUNKS):
        for d in (2, 1, 3):
            h = (y + d) % GROUP
            c_copies[d, c] = remote(
                bown.at[h, chunk(c)], brec.at[d, chunk(c)], c_s.at[d, c], c_r.at[d, c], row_dev(d)
            )
    gradient_state(y)

    def backward(h):
        go = goT[h]
        q_t = in_row(h) * nn(fent[h].astype(bf16), go)
        w0 = (nn(vh[h, 0:256, :], go) * decay[h, 0:256, :]).astype(bf16)
        w1 = (nn(vh[h, 256:512, :], go[:, 256:]) * decay[h, 256:512, 256:]).astype(bf16)
        q0 = q_t[:, 0:256] + nn(kT[h, :, 0:256], w0[:, 0:256])
        q1 = q_t[:, 256:] + nn(kT[h, :, 0:256], w0[:, 256:]) + nn(kT[h, :, 256:], w1)
        so_q[pl.ds(h, BLK, stride=HPD), :] = jnp.concatenate([q0.T, q1.T], axis=0)
        kacc[h, 0:256, :] = nn(w0, qh[h])
        kacc[h, 256:512, :] = nn(w1, qh[h, 256:512, :])
        vacc[h, 0:256, :] = nt(probsT[h, 0:256, :], go)
        vacc[h, 256:512, :] = nt(probsT[h, 256:512, 256:], go[:, 256:])

    drain(earlier)
    backward(0)
    backward(1)
    at = jnp.where(idx == 7, 0.0, idxf + 1.0)
    coefs = []
    for j in source:
        first_j = jnp.sum(jnp.where(idx == j, first_g, 0.0), axis=0, keepdims=True)
        jf = j.astype(f32)
        coefs.append(fade(rate_y, (jf >= at) & (first_j <= BLK * at), jf - at))
    u_copies = {}
    for c in range(CHUNKS):
        for d in (1, 3, 2):
            c_copies[d, c]()
        total_c = coefs[0][7:8, :] * bown[y, chunk(c), :]
        for d in range(1, GROUP):
            total_c = total_c + coefs[d][7:8, :] * brec[d, chunk(c), :]
        bsum[chunk(c), :] = total_c
        for n in (1, 0):
            u_copies[n, c] = remote(
                bsum.at[chunk(c)], bin_.at[n, chunk(c)], u_s.at[n, c], u_r.at[n, c], col_dev(-(n + 1)),
                pl.when(z > n), pl.when(z < zs - 1 - n),
            )
    for i in range(GROUP - 1):
        outer = coefs[0][i : i + 1, :] * bown[y]
        for d in range(1, GROUP):
            outer = outer + coefs[d][i : i + 1, :] * brec[d]
        bout[i] = outer
    backward(2)
    backward(3)
    oq[...] = so_q[0 : BLK * HPD, :].astype(bf16)
    far = fade(rate_y, first_g <= BLK * GROUP, jnp.full((8, 128), GROUP, f32))[6:7, :]
    carry = fade(rate_y, first_g[4:5, :] <= BLK * (idxf + 1.0), GROUP - 1.0 - idxf)
    earlier = sent[:]
    sent.clear()
    w_copies = {}
    for c in range(CHUNKS):
        for n in (0, 1):
            u_copies[n, c]()
        entry = bin_[0, chunk(c), :] + far * bin_[1, chunk(c), :]
        bout[GROUP - 1, chunk(c), :] = entry
        for i in range(GROUP - 1):
            bout[i, chunk(c), :] = bout[i, chunk(c), :] + carry[i : i + 1, :] * entry
        for d in (2, 1, 3):
            w_copies[d, c] = remote(
                bout.at[(y + d) % GROUP, chunk(c)], bent.at[y, chunk(c)], w_s.at[d, c], w_r.at[d, c], row_dev(d)
            )
    bent[y] = bout[y]
    drain(earlier)

    for d in (0, 1, 3, 2):
        h = source[d]
        if d:
            for c in range(CHUNKS):
                w_copies[d, c]()
        state = bent[h].astype(bf16)
        so_k[pl.ds(h, BLK, stride=HPD), :] = kacc[h] + backc[h] * nt(vh[h], state)
        so_v[pl.ds(h, BLK, stride=HPD), :] = vacc[h] + backc[h] * nn(kh[h], state)
    drain(sent)
    ok[...] = so_k[0 : BLK * HPD, :].astype(bf16)
    ov[...] = so_v[0 : BLK * HPD, :].astype(bf16)


def copy_out(a, b, c, a_hbm, b_hbm, c_hbm, sems):
    copies = [
        pltpu.make_async_copy(s, t, sems.at[i])
        for i, (s, t) in enumerate(((a, a_hbm), (b, b_hbm), (c, c_hbm)))
    ]
    for x in copies:
        x.start()
    for x in copies:
        x.wait()


def local(zs, hs, queries, keys, values, out_grad, gain, decay_rate, doc_lengths):
    rows = BLK * HPD
    flat = [a.reshape(rows, FEAT) for a in (queries, keys, values, out_grad)]
    hbm = pl.BlockSpec(memory_space=pltpu.HBM)
    vmem = pl.BlockSpec(memory_space=pltpu.VMEM)
    V = pltpu.VMEM
    mat = (FEAT, FEAT)
    chain = [
        V((HPD,) + mat, f32), V((GROUP,) + mat, f32), V(mat, f32),
        V((2,) + mat, f32), V((GROUP,) + mat, f32), V((HPD,) + mat, f32),
    ]
    scratch = (
        [V((rows, FEAT), bf16)] * 4
        + [V((rows + 8, FEAT), f32)] * 4
        + [V((HPD, BLK, FEAT), bf16)] * 3
        + [V((HPD, FEAT, BLK), bf16)] * 3
        + [V((HPD, FEAT, BLK), f32), V((BLK, BLK), f32), V((HPD, BLK, BLK), f32), V((HPD, BLK, BLK), bf16)]
        + [V((HPD, FEAT, BLK), f32), V((HPD, FEAT, BLK), bf16)]
        + chain + chain
        + [V((8, 128), f32), V((hs, 8, 128), f32)]
        + [V((HPD, BLK, FEAT), f32)] * 3
        + [V((rows + 8, FEAT), f32)] * 3
        + [V((HPD, FEAT), f32), pltpu.SMEM((1, HPD), f32), V((1, doc_lengths.shape[0]), jnp.int32)]
    )
    dma = pltpu.SemaphoreType.DMA
    moves = [dma((GROUP, CHUNKS))] * 2 + [dma((2, CHUNKS))] * 2 + [dma((GROUP, CHUNKS))] * 2
    sems = [dma((7,)), pltpu.SemaphoreType.REGULAR] + moves + [dma((hs,))] * 2 + moves
    operands = (*flat, gain, decay_rate.reshape(1, HPD), doc_lengths.reshape(1, doc_lengths.shape[0]))
    result = [jax.ShapeDtypeStruct((rows, FEAT), bf16)] * 3
    outs = pl.pallas_call(
        functools.partial(kernel, zs, hs, zs * GROUP * BLK, hs * HPD * FEAT),
        out_shape=[V((rows, FEAT), bf16)] * 3,
        in_specs=[hbm] * 7,
        out_specs=[vmem] * 3,
        scratch_shapes=scratch + sems,
        compiler_params=pltpu.CompilerParams(
            collective_id=0, has_side_effects=True, vmem_limit_bytes=40 * 2**20
        ),
        cost_estimate=pl.CostEstimate(flops=2 * 10**9, bytes_accessed=4 * 10**6, transcendentals=10**6),
    )(*(pltpu.with_memory_space_constraint(a, pltpu.HBM) for a in operands))
    outs = pl.pallas_call(
        copy_out, out_shape=result, in_specs=[vmem] * 3, out_specs=[hbm] * 3, scratch_shapes=[dma((3,))],
        compiler_params=pltpu.CompilerParams(vmem_limit_bytes=2**20),
    )(*outs)
    return tuple(o.reshape(BLK, HPD, FEAT) for o in outs)


def solution(mesh):
    spec = P("ctx", "head", None)
    zs, hs = mesh.shape["ctx"] // GROUP, mesh.shape["head"]
    return jax.shard_map(
        functools.partial(local, zs, hs), mesh=mesh,
        in_specs=(spec,) * 4 + (P("head", None), P("head"), P()),
        out_specs=(spec,) * 3, check_vma=False,
    )
```
